32 devices in a mesh: group: 2 (over y), dp: 8 (over z, x), blk: 2 (over core).
Axes of the slice: x: 2, y: 2, z: 4, core: 2. Of those that a mesh axis runs over, the one named last changes fastest.
Arguments:
- activations: bfloat16 [4096, 8192], P(('group', 'dp'), 'blk'), parts along dimension 0, may hold values from -6 to 6
- teacher_out: bfloat16 [4096, 8192], P(('group', 'dp'), 'blk'), parts along dimension 0, may hold values from -6 to 6
- block_order: int32 [64], replicated, may hold values from 0 to 63, each once
- gate_left: bfloat16 [64, 2048], P('blk', 'dp'), may hold values from -0.5 to 0.5
- gate_right: bfloat16 [64, 3584], P('blk', 'dp'), may hold values from -1.5 to 1.5
- up_left: bfloat16 [64, 2048], P('blk', 'dp'), may hold values from -0.5 to 0.5
- up_right: bfloat16 [64, 3584], P('blk', 'dp'), may hold values from -1.5 to 1.5
- down_left: bfloat16 [64, 3584], P('blk', 'dp'), may hold values from -0.375 to 0.375
- down_right: bfloat16 [64, 2048], P('blk', 'dp'), may hold values from -1.5 to 1.5
Outputs:
- grad_gate_left: float32 [128, 2048], P(('group', 'blk'), 'dp'), parts along dimension 0
- grad_gate_right: float32 [128, 3584], P(('group', 'blk'), 'dp'), parts along dimension 0
- grad_up_left: float32 [128, 2048], P(('group', 'blk'), 'dp'), parts along dimension 0
- grad_up_right: float32 [128, 3584], P(('group', 'blk'), 'dp'), parts along dimension 0
- grad_down_left: float32 [128, 3584], P(('group', 'blk'), 'dp'), parts along dimension 0
- grad_down_right: float32 [128, 2048], P(('group', 'blk'), 'dp'), parts along dimension 0
The draws below stay inside these ranges and needn't reach their ends.
There are 2 independent parts, one for each index of `group`. The reference program is written for one: setup_inputs(seed, part) draws one part's arguments, and reference() takes and returns one part's arrays. A program takes and returns all parts, laid end to end along the dimension named above; an argument that names none is the same for every part. Nothing has to cross between parts.
Inputs may be any that keep to these rules, and one draw needn't show every extreme that they name: block_order names each block exactly once.
All inputs are finite; a program needn't handle non-finite values.
Results may differ from the reference program's by a relative error of at most 0.0043.
Values may be sent and summed in bfloat16 or wider, within the bound.
No kernel may reach another device: no remote copies, remote signals or barrier semaphores. Data moves between devices by JAX's collectives and lax.ppermute only.
A program may use at most 128 MiB of HBM per device.

```python
import jax
import jax.numpy as jnp
from jax import lax

D = 8192
NB = 64
RANK = 16
TOK_DEV = 256
BIN = 128
BHID = 224
TOKENS = 2048
N_DP = 8


def level_of(rng, shape, pieces, smallest, high):
    def one(position, blocks):
        heights = jax.random.uniform(jax.random.fold_in(jax.random.fold_in(rng, 6), position), (blocks,), jnp.float32, smallest / len(pieces), high / len(pieces))
        return jnp.repeat(jnp.exp(heights), shape[position] // blocks).reshape((-1,) + (1,) * (len(shape) - position - 1))

    gain = one(*pieces[0])
    for cut in pieces[1:]:
        gain = gain * one(*cut)
    return gain


def gaussian(own_key, dims, scale, limit, cuts=(), dtype=jnp.bfloat16):
    values = jax.random.normal(own_key, dims, jnp.float32) * scale
    if len(cuts) > 0:
        values = level_of(own_key, dims, cuts, -0.22, 0.18) * values
    return jnp.clip(values, min=-limit, max=limit).astype(dtype)


def setup_inputs(seed: int = 0, part: int = 0) -> dict:
    seeds = jax.random.split(jax.random.key(seed), 10)
    part_splits = jax.random.split(jax.random.fold_in(seeds[9], part), 10)
    activations = gaussian(part_splits[0], (TOKENS, D), 1.0, 6.0, ((0, 8), (1, 2)))
    teacher_out = gaussian(part_splits[1], (TOKENS, D), 1.0, 6.0, ((0, 8), (1, 2)))
    block_order = jax.random.permutation(seeds[2], NB).astype(jnp.int32)
    gate_left = gaussian(seeds[3], (NB, BIN * RANK), BIN ** -0.5, 0.5, ((0, 2), (1, 8)))
    gate_right = gaussian(seeds[4], (NB, RANK * BHID), RANK ** -0.5, 1.5, ((0, 2), (1, 8)))
    up_left = gaussian(seeds[5], (NB, BIN * RANK), BIN ** -0.5, 0.5, ((0, 2), (1, 8)))
    up_right = gaussian(seeds[6], (NB, RANK * BHID), RANK ** -0.5, 1.5, ((0, 2), (1, 8)))
    down_left = gaussian(seeds[7], (NB, BHID * RANK), BHID ** -0.5, 0.375, ((0, 2), (1, 8)))
    down_right = gaussian(seeds[8], (NB, RANK * BIN), RANK ** -0.5, 1.5, ((0, 2), (1, 8)))
    return dict(activations=activations, teacher_out=teacher_out, block_order=block_order, gate_left=gate_left, gate_right=gate_right, up_left=up_left, up_right=up_right, down_left=down_left, down_right=down_right)


def mix(values, order):
    rows = values.shape[0]
    grid = values.reshape(rows, RANK, NB)
    return jnp.transpose(jnp.take(grid, order, axis=2), (0, 2, 1))


def unmix(values, order):
    rows = values.shape[0]
    inverse = jnp.argsort(order).astype(jnp.int32)
    grid = jnp.transpose(values, (0, 2, 1))
    return jnp.take(grid, inverse, axis=2).reshape(rows, NB, RANK)


def block_grads(inputs, target, order, gate_left, gate_right, up_left, up_right, down_left, down_right):
    f32 = jnp.float32
    bf16 = jnp.bfloat16
    rows = inputs.shape[0]
    feats = inputs.reshape(rows, NB, BIN).astype(f32)
    gate_inner = jnp.einsum('tjb,jbc->tjc', feats, gate_left.astype(f32)).astype(bf16)
    up_inner = jnp.einsum('tjb,jbc->tjc', feats, up_left.astype(f32)).astype(bf16)
    gate_mixed = mix(gate_inner, order)
    up_mixed = mix(up_inner, order)
    gate = jnp.einsum('tka,kao->tko', gate_mixed.astype(f32), gate_right.astype(f32))
    upper = jnp.einsum('tka,kao->tko', up_mixed.astype(f32), up_right.astype(f32))
    sig = jax.nn.sigmoid(gate)
    act = gate * sig
    hidden = (act * upper).astype(bf16)
    down_inner = jnp.einsum('tjo,joc->tjc', hidden.astype(f32), down_left.astype(f32)).astype(bf16)
    down_mixed = mix(down_inner, order)
    student = jnp.einsum('tka,kab->tkb', down_mixed.astype(f32), down_right.astype(f32))
    scale = float(TOKENS) ** -0.5
    delta = ((student - target.reshape(rows, NB, BIN).astype(f32)) * scale).astype(bf16)
    deltaf = delta.astype(f32)
    grad_rd = jnp.einsum('tka,tkb->kab', down_mixed.astype(f32), deltaf)
    down_back = jnp.einsum('tkb,kab->tka', deltaf, down_right.astype(f32)).astype(bf16)
    down_return = unmix(down_back, order).astype(f32)
    grad_ld = jnp.einsum('tjo,tjc->joc', hidden.astype(f32), down_return)
    dhidden = jnp.einsum('tjc,joc->tjo', down_return, down_left.astype(f32))
    dgate = (dhidden * upper * sig * (1.0 + gate * (1.0 - sig))).astype(bf16).astype(f32)
    dup = (dhidden * act).astype(bf16).astype(f32)
    grad_rg = jnp.einsum('tka,tko->kao', gate_mixed.astype(f32), dgate)
    grad_ru = jnp.einsum('tka,tko->kao', up_mixed.astype(f32), dup)
    gate_back = jnp.einsum('tko,kao->tka', dgate, gate_right.astype(f32)).astype(bf16)
    up_back = jnp.einsum('tko,kao->tka', dup, up_right.astype(f32)).astype(bf16)
    gate_return = unmix(gate_back, order).astype(f32)
    up_return = unmix(up_back, order).astype(f32)
    grad_lg = jnp.einsum('tjb,tjc->jbc', feats, gate_return)
    grad_lu = jnp.einsum('tjb,tjc->jbc', feats, up_return)
    return (grad_lg, grad_rg, grad_lu, grad_ru, grad_ld, grad_rd)


def reference(activations, teacher_out, block_order, gate_left, gate_right, up_left, up_right, down_left, down_right):
    f32 = jnp.float32
    factors = (gate_left.reshape(NB, BIN, RANK), gate_right.reshape(NB, RANK, BHID),
               up_left.reshape(NB, BIN, RANK), up_right.reshape(NB, RANK, BHID),
               down_left.reshape(NB, BHID, RANK), down_right.reshape(NB, RANK, BIN))
    inputs = activations.reshape(N_DP, TOK_DEV, D)
    targets = teacher_out.reshape(N_DP, TOK_DEV, D)
    zeros = (jnp.zeros((NB, BIN, RANK), f32), jnp.zeros((NB, RANK, BHID), f32),
             jnp.zeros((NB, BIN, RANK), f32), jnp.zeros((NB, RANK, BHID), f32),
             jnp.zeros((NB, BHID, RANK), f32), jnp.zeros((NB, RANK, BIN), f32))

    def step(carry, pair):
        terms = block_grads(pair[0], pair[1], block_order, *factors)
        return tuple(c + g for c, g in zip(carry, terms)), None

    totals, _ = lax.scan(step, zeros, (inputs, targets))
    return (totals[0].reshape(NB, -1), totals[1].reshape(NB, -1), totals[2].reshape(NB, -1),
            totals[3].reshape(NB, -1), totals[4].reshape(NB, -1), totals[5].reshape(NB, -1))
```

```python
import functools

import jax
import jax.numpy as jnp
from jax import lax
from jax.experimental import pallas as pl
from jax.experimental.pallas import tpu as pltpu
from jax.sharding import PartitionSpec as P

NB = 64
HALF = 32
RANK = 16
BIN = 128
BHID = 224
WIDE = 256
CHUNKS = 8
ROWS = 560
f32 = jnp.float32
bf16 = jnp.bfloat16

R_AT = 128
RD_AT = 384
LD_AT = 448


def pack(lg, rg, lu, ru, ld, rd):
    left = jnp.stack([lg, lu]).reshape(2, HALF, 16, 2, 8)
    left = jnp.transpose(left, (2, 4, 3, 0, 1)).reshape(128, 128)
    right = jnp.stack([rg, ru]).reshape(2, HALF, 2, BHID)
    right = jnp.pad(right, ((0, 0), (0, 0), (0, 0), (0, WIDE - BHID)))
    right = right.reshape(2, HALF, 2, 2, 128)
    right = jnp.transpose(right, (3, 0, 2, 1, 4)).reshape(256, 128)
    rdown = jnp.transpose(rd.reshape(HALF, 2, 128), (1, 0, 2)).reshape(64, 128)
    ldown = jnp.transpose(ld.reshape(HALF, 28, 4, 4), (1, 3, 2, 0)).reshape(112, 128)
    return jnp.concatenate([left, right, rdown, ldown], axis=0)


def unpack(packed):
    left = packed[:R_AT].reshape(16, 8, 2, 2, HALF)
    left = jnp.transpose(left, (3, 4, 0, 2, 1)).reshape(2, HALF, 256)
    right = packed[R_AT:RD_AT].reshape(2, 2, 2, HALF, 128)
    right = jnp.transpose(right, (1, 3, 2, 0, 4)).reshape(2, HALF, 2, WIDE)
    right = right[..., :BHID].reshape(2, HALF, 448)
    rdown = jnp.transpose(packed[RD_AT:LD_AT].reshape(2, HALF, 128), (1, 0, 2)).reshape(HALF, 256)
    ldown = packed[LD_AT:].reshape(28, 4, 4, HALF)
    ldown = jnp.transpose(ldown, (3, 0, 2, 1)).reshape(HALF, 448)
    return left[0], right[0], left[1], right[1], ldown, rdown


def nn(a, b):
    return jnp.dot(a, b, preferred_element_type=f32)


def nt(a, b):
    return lax.dot_general(a, b, (((1,), (1,)), ((), ())), preferred_element_type=f32)


def rounded(v):
    return v.astype(bf16).astype(f32)


def wide(pair, row, stride):
    return jnp.concatenate([v[pl.ds(row, RANK, stride=stride), :] for v in pair], axis=1).astype(bf16)


def widen(pair, row, stride, value):
    pair[0][pl.ds(row, RANK, stride=stride), :] = value[:, :128]
    pair[1][pl.ds(row, RANK, stride=stride), :] = value[:, 128:]


def body(scale, where, order, *refs):
    weights = refs[:16]
    x_ref, y_ref, out_ref = refs[16:19]
    (s_l, r_lo, r_hi, s_rd, d_lo, d_hi, inner, down, ret, act_s, slope_s, hid_s, stage) = refs[19:]
    s_r = (r_lo, r_hi)
    s_ld = (d_lo, d_hi)
    toks = x_ref.shape[0]
    me = where[0]
    side = where[1]

    for own in range(2):
        blk = side if own == 0 else 1 - side
        for r in range(CHUNKS):
            g = weights[own * CHUNKS + r]
            d = me ^ r
            for gu in range(2):
                for al in range(2):
                    row = pl.multiple_of((2 * d + al) * 128 + gu * NB + blk * HALF, HALF)
                    for half in range(2):
                        at = R_AT + half * 128 + gu * 64 + al * HALF
                        s_r[half][pl.ds(row, HALF), :] = g[pl.ds(at, HALF), :].astype(f32)
            for al in range(2):
                row = pl.multiple_of((2 * d + al) * NB + blk * HALF, HALF)
                s_rd[pl.ds(row, HALF), :] = g[pl.ds(RD_AT + al * HALF, HALF), :].astype(f32)
            stage[pl.ds(pl.multiple_of(d * 128, 128), 128), :] = g[pl.ds(0, 128), :].astype(f32)
            stage[pl.ds(pl.multiple_of(1024 + d * 112, 16), 112), :] = g[pl.ds(LD_AT, 112), :].astype(f32)
        for c8 in range(8):
            t = stage[pl.ds(c8, 128, stride=8), :].T
            for ch in range(2):
                for gu in range(2):
                    row = pl.multiple_of((ch * 8 + c8) * 128 + gu * NB + blk * HALF, HALF)
                    s_l[pl.ds(row, HALF), :] = t[(ch * 2 + gu) * HALF : (ch * 2 + gu + 1) * HALF]
        for c4 in range(4):
            t0 = stage[pl.ds(1024 + c4, 128, stride=4), :].T
            t1 = stage[pl.ds(1024 + 512 + c4, 96, stride=4), :]
            t1 = jnp.concatenate([t1, jnp.zeros((32, 128), f32)], axis=0).T
            for cq in range(4):
                row = pl.multiple_of((cq * 4 + c4) * NB + blk * HALF, HALF)
                d_lo[pl.ds(row, HALF), :] = t0[cq * HALF : (cq + 1) * HALF]
                d_hi[pl.ds(row, HALF), :] = t1[cq * HALF : (cq + 1) * HALF]

    def lanes(j, width=BIN):
        return pl.ds(pl.multiple_of(j * width, width), width)

    def first(j, _):
        wg = s_l[pl.ds(j, RANK, stride=128), :]
        wu = s_l[pl.ds(j + NB, RANK, stride=128), :]
        w = jnp.concatenate([wg, wu], axis=0).astype(bf16)
        got = rounded(nt(w, x_ref[:, lanes(j)]))
        at = pl.multiple_of(j * RANK, RANK)
        inner[pl.ds(at, RANK), :] = got[:RANK]
        inner[pl.ds(1024 + at, RANK), :] = got[RANK:]
        return 0

    lax.fori_loop(0, NB, first, 0, unroll=4)

    def mixed_of(m):
        return jnp.concatenate(
            [inner[pl.ds(m, RANK, stride=NB), :], inner[pl.ds(1024 + m, RANK, stride=NB), :]], axis=0
        )

    zeros = jnp.zeros((RANK, WIDE), bf16)

    def second(k, _):
        m = order[k]
        mixed = mixed_of(m).T.astype(bf16)
        wg = wide(s_r, k, 128)
        wu = wide(s_r, k + NB, 128)
        gate = nn(mixed, jnp.concatenate([wg, zeros], axis=0))
        upper = nn(mixed, jnp.concatenate([zeros, wu], axis=0))
        sig = 1.0 / (1.0 + jnp.exp(-gate))
        act = gate * sig
        hidden = (act * upper).astype(bf16)
        act_s[k] = act
        slope_s[k] = upper * sig * (1.0 + gate * (1.0 - sig))
        hid_s[k] = hidden
        wl = wide(s_ld, k, NB)
        down[pl.ds(pl.multiple_of(k * RANK, RANK), RANK), :] = rounded(nt(wl, hidden))
        return 0

    lax.fori_loop(0, NB, second, 0, unroll=2)

    def third(k, _):
        m = order[k]
        dm = down[pl.ds(m, RANK, stride=NB), :]
        wr = s_rd[pl.ds(k, RANK, stride=NB), :].astype(bf16)
        student = nn(dm.T.astype(bf16), wr)
        delta = ((student - y_ref[:, lanes(k)].astype(f32)) * scale).astype(bf16)
        back = rounded(nt(wr, delta))
        s_rd[pl.ds(k, RANK, stride=NB), :] = nn(dm.astype(bf16), delta)
        ret[pl.ds(m, RANK, stride=NB), :] = back
        return 0

    lax.fori_loop(0, NB, third, 0, unroll=2)

    def fourth(j, _):
        m = order[j]
        dr = ret[pl.ds(pl.multiple_of(j * RANK, RANK), RANK), :]
        wl = wide(s_ld, j, NB)
        dhidden = nn(dr.T.astype(bf16), wl)
        widen(s_ld, j, NB, nn(dr.astype(bf16), hid_s[j]))
        dgate = (dhidden * slope_s[j]).astype(bf16)
        dup = (dhidden * act_s[j]).astype(bf16)
        gm = inner[pl.ds(m, RANK, stride=NB), :].astype(bf16)
        um = inner[pl.ds(1024 + m, RANK, stride=NB), :].astype(bf16)
        wg = wide(s_r, j, 128)
        wu = wide(s_r, j + NB, 128)
        inner[pl.ds(m, RANK, stride=NB), :] = rounded(nt(wg, dgate))
        inner[pl.ds(1024 + m, RANK, stride=NB), :] = rounded(nt(wu, dup))
        widen(s_r, j, 128, nn(gm, dgate))
        widen(s_r, j + NB, 128, nn(um, dup))
        return 0

    lax.fori_loop(0, NB, fourth, 0, unroll=2)

    def fifth(j, _):
        at = pl.multiple_of(j * RANK, RANK)
        back = jnp.concatenate([inner[pl.ds(at, RANK), :], inner[pl.ds(1024 + at, RANK), :]], axis=0)
        grads = nn(back.astype(bf16), x_ref[:, lanes(j)])
        s_l[pl.ds(j, RANK, stride=128), :] = grads[:RANK]
        s_l[pl.ds(j + NB, RANK, stride=128), :] = grads[RANK:]
        return 0

    lax.fori_loop(0, NB, fifth, 0, unroll=4)

    for blk in range(2):
        for c8 in range(8):
            parts = []
            for ch in range(2):
                for gu in range(2):
                    row = (ch * 8 + c8) * 128 + gu * NB + blk * HALF
                    parts.append(s_l[pl.ds(row, HALF), :])
            stage[pl.ds(c8, 128, stride=8), :] = jnp.concatenate(parts, axis=0).T
        for c4 in range(4):
            p0, p1 = [], []
            for cq in range(4):
                row = (cq * 4 + c4) * NB + blk * HALF
                p0.append(d_lo[pl.ds(row, HALF), :])
                p1.append(d_hi[pl.ds(row, HALF), :])
            stage[pl.ds(1024 + c4, 128, stride=4), :] = jnp.concatenate(p0, axis=0).T
            stage[pl.ds(1024 + 512 + c4, 96, stride=4), :] = jnp.concatenate(p1, axis=0).T[:96]
        for d in range(CHUNKS):
            out_ref[blk, d, pl.ds(0, 128), :] = stage[pl.ds(d * 128, 128), :].astype(bf16)
            out_ref[blk, d, pl.ds(LD_AT, 112), :] = stage[pl.ds(1024 + d * 112, 112), :].astype(bf16)
            for gu in range(2):
                for al in range(2):
                    row = (2 * d + al) * 128 + gu * NB + blk * HALF
                    for half in range(2):
                        at = R_AT + half * 128 + gu * 64 + al * HALF
                        out_ref[blk, d, pl.ds(at, HALF), :] = s_r[half][pl.ds(row, HALF), :].astype(bf16)
            for al in range(2):
                row = (2 * d + al) * NB + blk * HALF
                out_ref[blk, d, pl.ds(RD_AT + al * HALF, HALF), :] = s_rd[pl.ds(row, HALF), :].astype(bf16)


def layer(scale, where, order, weights, x, y):
    toks = x.shape[0]
    vmem = pl.BlockSpec(memory_space=pltpu.VMEM)
    smem = pl.BlockSpec(memory_space=pltpu.SMEM)
    return pl.pallas_call(
        functools.partial(body, scale),
        out_shape=jax.ShapeDtypeStruct((2, CHUNKS, ROWS, 128), bf16),
        in_specs=[smem, smem] + [vmem] * 18,
        out_specs=vmem,
        scratch_shapes=[
            pltpu.VMEM((RANK * 128, BIN), f32),
            pltpu.VMEM((RANK * 128, 128), f32),
            pltpu.VMEM((RANK * 128, 128), f32),
            pltpu.VMEM((RANK * NB, BIN), f32),
            pltpu.VMEM((RANK * NB, 128), f32),
            pltpu.VMEM((RANK * NB, 128), f32),
            pltpu.VMEM((2 * NB * RANK, toks), f32),
            pltpu.VMEM((NB * RANK, toks), f32),
            pltpu.VMEM((NB * RANK, toks), f32),
            pltpu.VMEM((NB, toks, WIDE), f32),
            pltpu.VMEM((NB, toks, WIDE), f32),
            pltpu.VMEM((NB, toks, WIDE), bf16),
            pltpu.VMEM((1024 + 896, 128), f32),
        ],
        compiler_params=pltpu.CompilerParams(vmem_limit_bytes=56 * 2**20),
    )(where, order, *weights, x, y)


def swap(v, axis, bit, size):
    return lax.ppermute(v, axis, [(i, i ^ bit) for i in range(size)])


def at(v, i):
    return lax.dynamic_index_in_dim(v, i, 0, keepdims=False)


def tokens_of(v, side):
    half = v.shape[0] // 2
    own = lax.dynamic_slice_in_dim(v, side * half, half, 0)
    sent = lax.dynamic_slice_in_dim(v, (1 - side) * half, half, 0)
    got = swap(sent, "blk", 1, 2)
    first = jnp.where(side == 0, own, got)
    second = jnp.where(side == 0, got, own)
    return jnp.concatenate([first, second], axis=1)


def on_device(activations, teacher_out, block_order, *factors):
    n = lax.axis_size("dp")
    me = lax.axis_index("dp")
    side = lax.axis_index("blk")
    scale = float(activations.shape[0] * n) ** (-0.5)
    x = tokens_of(activations, side)
    y = tokens_of(teacher_out, side)
    if n == CHUNKS:
        mine = pack(*factors)
        along = [mine] + [swap(mine, "dp", 2 * s, n) for s in range(1, 4)]
        own = []
        for piece in along:
            own += [piece, swap(piece, "dp", 1, n)]
        where = jnp.stack([me, side]).astype(jnp.int32)
    else:
        whole = [lax.all_gather(v, "dp", axis=1, tiled=True) for v in factors]
        cut = [jnp.moveaxis(v.reshape(HALF, CHUNKS, -1), 1, 0) for v in whole]
        packed = jax.vmap(pack)(*cut)
        own = [packed[d] for d in range(CHUNKS)]
        where = jnp.stack([jnp.zeros_like(side), side]).astype(jnp.int32)
    other = swap(jnp.stack(own), "blk", 1, 2)
    grads = layer(scale, where, block_order, own + [other[d] for d in range(CHUNKS)], x, y)
    total = at(grads, side).astype(f32) + swap(at(grads, 1 - side), "blk", 1, 2).astype(f32)
    if n == CHUNKS:
        total = total.astype(bf16).reshape(4, 2, ROWS, 128)
        xs, zs = me % 2, me // 2
        pick = functools.partial(lax.dynamic_index_in_dim, axis=1, keepdims=False)
        line = pick(total, xs).astype(f32) + swap(pick(total, 1 - xs), "dp", 1, n).astype(f32)
        line = line.astype(bf16)
        result = at(line, zs).astype(f32)
        for s in range(1, 4):
            result = result + swap(at(line, zs ^ s), "dp", 2 * s, n).astype(f32)
        return unpack(result)
    parts = jax.vmap(unpack)(total)
    parts = [jnp.moveaxis(v, 0, 1).reshape(HALF, -1) for v in parts]
    return tuple(lax.psum_scatter(v, "dp", scatter_dimension=1, tiled=True) for v in parts)


def solution(mesh):
    rows = P(("group", "dp"), "blk")
    factor = P("blk", "dp")
    grad = P(("group", "blk"), "dp")
    return jax.shard_map(
        on_device,
        mesh=mesh,
        in_specs=(rows, rows, P()) + (factor,) * 6,
        out_specs=(grad,) * 6,
        check_vma=False,
    )
```

```python
import functools

import jax
import jax.numpy as jnp
from jax import lax
from jax.experimental import pallas as pl
from jax.experimental.pallas import tpu as pltpu
from jax.sharding import PartitionSpec as P

NB = 64
HALF = 32
RANK = 16
BIN = 128
BHID = 224
WIDE = 256
CHUNKS = 8
GROUP = 8
ROWS = 560
f32 = jnp.float32
bf16 = jnp.bfloat16

R_AT = 128
RD_AT = 384
LD_AT = 448


def pack(lg, rg, lu, ru, ld, rd):
    left = jnp.stack([lg, lu]).reshape(2, HALF, 16, 2, 8)
    left = jnp.transpose(left, (2, 4, 3, 0, 1)).reshape(128, 128)
    right = jnp.stack([rg, ru]).reshape(2, HALF, 2, BHID)
    right = jnp.pad(right, ((0, 0), (0, 0), (0, 0), (0, WIDE - BHID)))
    right = right.reshape(2, HALF, 2, 2, 128)
    right = jnp.transpose(right, (3, 0, 2, 1, 4)).reshape(256, 128)
    rdown = jnp.transpose(rd.reshape(HALF, 2, 128), (1, 0, 2)).reshape(64, 128)
    ldown = jnp.transpose(ld.reshape(HALF, 28, 4, 4), (1, 3, 2, 0)).reshape(112, 128)
    return jnp.concatenate([left, right, rdown, ldown], axis=0)


def unpack(packed):
    left = packed[:R_AT].reshape(16, 8, 2, 2, HALF)
    left = jnp.transpose(left, (3, 4, 0, 2, 1)).reshape(2, HALF, 256)
    right = packed[R_AT:RD_AT].reshape(2, 2, 2, HALF, 128)
    right = jnp.transpose(right, (1, 3, 2, 0, 4)).reshape(2, HALF, 2, WIDE)
    right = right[..., :BHID].reshape(2, HALF, 448)
    rdown = jnp.transpose(packed[RD_AT:LD_AT].reshape(2, HALF, 128), (1, 0, 2)).reshape(HALF, 256)
    ldown = packed[LD_AT:].reshape(28, 4, 4, HALF)
    ldown = jnp.transpose(ldown, (3, 0, 2, 1)).reshape(HALF, 448)
    return left[0], right[0], left[1], right[1], ldown, rdown


def nn(a, b):
    return jnp.dot(a, b, preferred_element_type=f32)


def nt(a, b):
    return lax.dot_general(a, b, (((1,), (1,)), ((), ())), preferred_element_type=f32)


def rounded(v):
    return v.astype(bf16).astype(f32)


def wide(pair, row, stride):
    return jnp.concatenate([v[pl.ds(row, RANK, stride=stride), :] for v in pair], axis=1).astype(bf16)


def widen(pair, row, stride, value):
    pair[0][pl.ds(row, RANK, stride=stride), :] = value[:, :128]
    pair[1][pl.ds(row, RANK, stride=stride), :] = value[:, 128:]


def body(scale, where, order, *refs):
    weights = refs[:16]
    x_ref, y_ref, out_ref = refs[16:19]
    (s_l, r_lo, r_hi, s_rd, d_lo, d_hi, g_l, q_lo, q_hi, g_rd, e_lo, e_hi,
     inner, back, down, ret, act_s, slope_s, hid_s, stage,
     t_l, t_r, t_rd, t_ld) = refs[19:]
    s_r = (r_lo, r_hi)
    s_ld = (d_lo, d_hi)
    g_r = (q_lo, q_hi)
    g_ld = (e_lo, e_hi)
    toks = x_ref.shape[0]
    me = where[0]
    side = where[1]

    for own in range(2):
        blk = side if own == 0 else 1 - side
        for r in range(CHUNKS):
            g = weights[own * CHUNKS + r]
            d = me ^ r
            for gu in range(2):
                for al in range(2):
                    row = pl.multiple_of((2 * d + al) * 128 + gu * NB + blk * HALF, HALF)
                    for half in range(2):
                        at = R_AT + half * 128 + gu * 64 + al * HALF
                        s_r[half][pl.ds(row, HALF), :] = g[pl.ds(at, HALF), :].astype(f32)
            for al in range(2):
                row = pl.multiple_of((2 * d + al) * NB + blk * HALF, HALF)
                s_rd[pl.ds(row, HALF), :] = g[pl.ds(RD_AT + al * HALF, HALF), :].astype(f32)
            stage[pl.ds(pl.multiple_of(d * 128, 128), 128), :] = g[pl.ds(0, 128), :].astype(f32)
            stage[pl.ds(pl.multiple_of(1024 + d * 112, 16), 112), :] = g[pl.ds(LD_AT, 112), :].astype(f32)
        for c8 in range(8):
            t = stage[pl.ds(c8, 128, stride=8), :].T
            for ch in range(2):
                for gu in range(2):
                    row = pl.multiple_of((ch * 8 + c8) * 128 + gu * NB + blk * HALF, HALF)
                    s_l[pl.ds(row, HALF), :] = t[(ch * 2 + gu) * HALF : (ch * 2 + gu + 1) * HALF]
        for c4 in range(4):
            t0 = stage[pl.ds(1024 + c4, 128, stride=4), :].T
            t1 = stage[pl.ds(1024 + 512 + c4, 96, stride=4), :]
            t1 = jnp.concatenate([t1, jnp.zeros((32, 128), f32)], axis=0).T
            for cq in range(4):
                row = pl.multiple_of((cq * 4 + c4) * NB + blk * HALF, HALF)
                d_lo[pl.ds(row, HALF), :] = t0[cq * HALF : (cq + 1) * HALF]
                d_hi[pl.ds(row, HALF), :] = t1[cq * HALF : (cq + 1) * HALF]

    def lanes(j, width=BIN):
        return pl.ds(pl.multiple_of(j * width, width), width)

    def rows(j, height=RANK):
        return pl.ds(pl.multiple_of(j * height, height), height)

    slot = lax.broadcasted_iota(jnp.int32, (1, 128), 1) // RANK
    masks = [jnp.where(slot == u, 1.0, 0.0).astype(bf16) for u in range(GROUP)]

    def stacked(ref, start, stride, g):
        return jnp.concatenate(
            [ref[pl.ds(start + g * GROUP + u, RANK, stride=stride), :] for u in range(GROUP)], axis=0
        )

    def turn(g, _):
        for gu in range(2):
            t_l[gu, g] = stacked(s_l, gu * NB, 128, g).T.astype(bf16)
            for h in range(2):
                t_r[gu, g, pl.ds(h * 128, 128), :] = stacked(s_r[h], gu * NB, 128, g).T.astype(bf16)
        for h in range(2):
            t_ld[g, pl.ds(h * 128, 128), :] = stacked(s_ld[h], 0, NB, g).T.astype(bf16)
        t_rd[g] = stacked(s_rd, 0, NB, g).T.astype(bf16)
        return 0

    lax.fori_loop(0, NB // GROUP, turn, 0)

    def blocks(g):
        return [(u, g * GROUP + u) for u in range(GROUP)]

    def first(g, _):
        for gu in range(2):
            total = jnp.zeros((toks, 128), f32)
            for u, j in blocks(g):
                total += nn(x_ref[:, lanes(j)], t_l[gu, g] * masks[u])
            inner[rows(gu * GROUP + g, 128), :] = rounded(total.T)
        return 0

    lax.fori_loop(0, NB // GROUP, first, 0)

    def second(g, _):
        turned = []
        for gu in range(2):
            mixed = [inner[pl.ds(gu * 1024 + order[k], RANK, stride=NB), :] for u, k in blocks(g)]
            turned.append(jnp.concatenate(mixed, axis=0).T.astype(bf16))
        for u, k in blocks(g):
            at = u * RANK
            act_s[k] = nn(turned[0][:, at : at + RANK], wide(s_r, k, 128))
            slope_s[k] = nn(turned[1][:, at : at + RANK], wide(s_r, k + NB, 128))
        for u, k in blocks(g):
            gate, upper = act_s[k], slope_s[k]
            sig = 0.5 * jnp.tanh(0.5 * gate) + 0.5
            act = gate * sig
            act_s[k] = act
            slope_s[k] = upper * (sig + act * (1.0 - sig))
            hid_s[k] = (act * upper).astype(bf16)
        total = jnp.zeros((toks, 128), f32)
        for u, k in blocks(g):
            total += nn(hid_s[k], t_ld[g] * masks[u])
        down[rows(g, 128), :] = rounded(total.T)
        return 0

    lax.fori_loop(0, NB // GROUP, second, 0)

    def third(g, _):
        dms = [down[pl.ds(order[k], RANK, stride=NB), :] for u, k in blocks(g)]
        turned = jnp.concatenate(dms, axis=0).T.astype(bf16)
        deltas = []
        for u, k in blocks(g):
            wr = s_rd[pl.ds(k, RANK, stride=NB), :].astype(bf16)
            student = nn(turned[:, u * RANK : (u + 1) * RANK], wr)
            deltas.append(((student - y_ref[:, lanes(k)].astype(f32)) * scale).astype(bf16))
        total = jnp.zeros((toks, 128), f32)
        for u, k in blocks(g):
            total += nn(deltas[u], t_rd[g] * masks[u])
        for u, k in blocks(g):
            g_rd[pl.ds(k, RANK, stride=NB), :] = nn(dms[u].astype(bf16), deltas[u])
        total = rounded(total.T)
        for u, k in blocks(g):
            ret[pl.ds(order[k], RANK, stride=NB), :] = total[u * RANK : (u + 1) * RANK]
        return 0

    lax.fori_loop(0, NB // GROUP, third, 0)

    def fourth(g, _):
        returned = ret[rows(g, 128), :]
        turned = returned.T.astype(bf16)
        for u, j in blocks(g):
            widen(g_ld, j, NB, nn(returned[u * RANK : (u + 1) * RANK].astype(bf16), hid_s[j]))
        sent = []
        for u, j in blocks(g):
            dhidden = nn(turned[:, u * RANK : (u + 1) * RANK], wide(s_ld, j, NB))
            sent.append(((dhidden * slope_s[j]).astype(bf16), (dhidden * act_s[j]).astype(bf16)))
        for gu in range(2):
            total = jnp.zeros((toks, 128), f32)
            for u, j in blocks(g):
                total += nn(sent[u][gu], t_r[gu, g] * masks[u])
            total = rounded(total.T)
            for u, j in blocks(g):
                back[pl.ds(gu * 1024 + order[j], RANK, stride=NB), :] = total[u * RANK : (u + 1) * RANK]
            for u, j in blocks(g):
                mixed = inner[pl.ds(gu * 1024 + order[j], RANK, stride=NB), :].astype(bf16)
                widen(g_r, j + gu * NB, 128, nn(mixed, sent[u][gu]))
        return 0

    lax.fori_loop(0, NB // GROUP, fourth, 0)

    def fifth(g, _):
        for u, j in blocks(g):
            both = jnp.concatenate([back[rows(j), :], back[rows(j + NB), :]], axis=0)
            grads = nn(both.astype(bf16), x_ref[:, lanes(j)])
            g_l[pl.ds(j, RANK, stride=128), :] = grads[:RANK]
            g_l[pl.ds(j + NB, RANK, stride=128), :] = grads[RANK:]
        return 0

    lax.fori_loop(0, NB // GROUP, fifth, 0)

    for blk in range(2):
        for c8 in range(8):
            parts = []
            for ch in range(2):
                for gu in range(2):
                    row = (ch * 8 + c8) * 128 + gu * NB + blk * HALF
                    parts.append(g_l[pl.ds(row, HALF), :])
            stage[pl.ds(c8, 128, stride=8), :] = jnp.concatenate(parts, axis=0).T
        for c4 in range(4):
            p0, p1 = [], []
            for cq in range(4):
                row = (cq * 4 + c4) * NB + blk * HALF
                p0.append(e_lo[pl.ds(row, HALF), :])
                p1.append(e_hi[pl.ds(row, HALF), :])
            stage[pl.ds(1024 + c4, 128, stride=4), :] = jnp.concatenate(p0, axis=0).T
            stage[pl.ds(1024 + 512 + c4, 96, stride=4), :] = jnp.concatenate(p1, axis=0).T[:96]
        for d in range(CHUNKS):
            out_ref[blk, d, pl.ds(0, 128), :] = stage[pl.ds(d * 128, 128), :].astype(bf16)
            out_ref[blk, d, pl.ds(LD_AT, 112), :] = stage[pl.ds(1024 + d * 112, 112), :].astype(bf16)
            for gu in range(2):
                for al in range(2):
                    row = (2 * d + al) * 128 + gu * NB + blk * HALF
                    for half in range(2):
                        at = R_AT + half * 128 + gu * 64 + al * HALF
                        out_ref[blk, d, pl.ds(at, HALF), :] = g_r[half][pl.ds(row, HALF), :].astype(bf16)
            for al in range(2):
                row = (2 * d + al) * NB + blk * HALF
                out_ref[blk, d, pl.ds(RD_AT + al * HALF, HALF), :] = g_rd[pl.ds(row, HALF), :].astype(bf16)


def layer(scale, where, order, weights, x, y):
    toks = x.shape[0]
    vmem = pl.BlockSpec(memory_space=pltpu.VMEM)
    smem = pl.BlockSpec(memory_space=pltpu.SMEM)
    return pl.pallas_call(
        functools.partial(body, scale),
        out_shape=jax.ShapeDtypeStruct((2, CHUNKS, ROWS, 128), bf16),
        in_specs=[smem, smem] + [vmem] * 18,
        out_specs=vmem,
        scratch_shapes=[
            pltpu.VMEM((RANK * 128, BIN), f32),
            pltpu.VMEM((RANK * 128, 128), f32),
            pltpu.VMEM((RANK * 128, 128), f32),
            pltpu.VMEM((RANK * NB, BIN), f32),
            pltpu.VMEM((RANK * NB, 128), f32),
            pltpu.VMEM((RANK * NB, 128), f32),
            pltpu.VMEM((RANK * 128, BIN), f32),
            pltpu.VMEM((RANK * 128, 128), f32),
            pltpu.VMEM((RANK * 128, 128), f32),
            pltpu.VMEM((RANK * NB, BIN), f32),
            pltpu.VMEM((RANK * NB, 128), f32),
            pltpu.VMEM((RANK * NB, 128), f32),
            pltpu.VMEM((2 * NB * RANK, toks), f32),
            pltpu.VMEM((2 * NB * RANK, toks), f32),
            pltpu.VMEM((NB * RANK, toks), f32),
            pltpu.VMEM((NB * RANK, toks), f32),
            pltpu.VMEM((NB, toks, WIDE), f32),
            pltpu.VMEM((NB, toks, WIDE), f32),
            pltpu.VMEM((NB, toks, WIDE), bf16),
            pltpu.VMEM((1024 + 896, 128), f32),
            pltpu.VMEM((2, NB // GROUP, BIN, 128), bf16),
            pltpu.VMEM((2, NB // GROUP, WIDE, 128), bf16),
            pltpu.VMEM((NB // GROUP, BIN, 128), bf16),
            pltpu.VMEM((NB // GROUP, WIDE, 128), bf16),
        ],
        compiler_params=pltpu.CompilerParams(vmem_limit_bytes=56 * 2**20),
    )(where, order, *weights, x, y)


def swap(v, axis, bit, size):
    return lax.ppermute(v, axis, [(i, i ^ bit) for i in range(size)])


def at(v, i):
    return lax.dynamic_index_in_dim(v, i, 0, keepdims=False)


def tokens_of(v, side):
    half = v.shape[0] // 2
    own = lax.dynamic_slice_in_dim(v, side * half, half, 0)
    sent = lax.dynamic_slice_in_dim(v, (1 - side) * half, half, 0)
    got = swap(sent, "blk", 1, 2)
    first = jnp.where(side == 0, own, got)
    second = jnp.where(side == 0, got, own)
    return jnp.concatenate([first, second], axis=1)


def on_device(activations, teacher_out, block_order, *factors):
    n = lax.axis_size("dp")
    me = lax.axis_index("dp")
    side = lax.axis_index("blk")
    scale = float(activations.shape[0] * n) ** (-0.5)
    x = tokens_of(activations, side)
    y = tokens_of(teacher_out, side)
    if n == CHUNKS:
        mine = pack(*factors)
        along = [mine] + [swap(mine, "dp", 2 * s, n) for s in range(1, 4)]
        own = []
        for piece in along:
            own += [piece, swap(piece, "dp", 1, n)]
        where = jnp.stack([me, side]).astype(jnp.int32)
    else:
        whole = [lax.all_gather(v, "dp", axis=1, tiled=True) for v in factors]
        cut = [jnp.moveaxis(v.reshape(HALF, CHUNKS, -1), 1, 0) for v in whole]
        packed = jax.vmap(pack)(*cut)
        own = [packed[d] for d in range(CHUNKS)]
        where = jnp.stack([jnp.zeros_like(side), side]).astype(jnp.int32)
    other = swap(jnp.stack(own), "blk", 1, 2)
    grads = layer(scale, where, block_order, own + [other[d] for d in range(CHUNKS)], x, y)
    total = at(grads, side).astype(f32) + swap(at(grads, 1 - side), "blk", 1, 2).astype(f32)
    if n == CHUNKS:
        total = total.astype(bf16).reshape(4, 2, ROWS, 128)
        xs, zs = me % 2, me // 2
        pick = functools.partial(lax.dynamic_index_in_dim, axis=1, keepdims=False)
        line = pick(total, xs).astype(f32) + swap(pick(total, 1 - xs), "dp", 1, n).astype(f32)
        line = line.astype(bf16)
        result = at(line, zs).astype(f32)
        for s in range(1, 4):
            result = result + swap(at(line, zs ^ s), "dp", 2 * s, n).astype(f32)
        return unpack(result)
    parts = jax.vmap(unpack)(total)
    parts = [jnp.moveaxis(v, 0, 1).reshape(HALF, -1) for v in parts]
    return tuple(lax.psum_scatter(v, "dp", scatter_dimension=1, tiled=True) for v in parts)


def solution(mesh):
    rows = P(("group", "dp"), "blk")
    factor = P("blk", "dp")
    grad = P(("group", "blk"), "dp")
    return jax.shard_map(
        on_device,
        mesh=mesh,
        in_specs=(rows, rows, P()) + (factor,) * 6,
        out_specs=(grad,) * 6,
        check_vma=False,
    )
```

```python
import functools

import jax
import jax.numpy as jnp
from jax import lax
from jax.experimental import pallas as pl
from jax.experimental.pallas import tpu as pltpu
from jax.sharding import PartitionSpec as P

NB = 64
HALF = 32
RANK = 16
BIN = 128
BHID = 224
WIDE = 256
CHUNKS = 8
GROUP = 8
GROUPS = NB // GROUP
f32 = jnp.float32
bf16 = jnp.bfloat16

FIRST = 128
REST = 448
RD_AT = 256
LD_AT = 320
RIGHT = 256
DOWN = 192


def pack(lg, rg, lu, ru, ld, rd):
    left = jnp.stack([lg, lu]).reshape(2, 4, 8, 16, 16)
    left = jnp.transpose(left, (0, 1, 3, 2, 4)).reshape(FIRST, 128)
    right = jnp.stack([rg, ru]).reshape(2, HALF, 2, 8, 28)
    right = jnp.pad(right, ((0, 0),) * 4 + ((0, 4),)).reshape(2, HALF, 2, 2, 128)
    right = jnp.transpose(right, (3, 0, 2, 1, 4)).reshape(256, 128)
    rdown = jnp.transpose(rd.reshape(HALF, 2, 128), (1, 0, 2)).reshape(64, 128)
    ldown = jnp.transpose(ld.reshape(4, 8, 28, 16), (0, 2, 1, 3)).reshape(4, 28, 128)
    ldown = jnp.pad(ldown, ((0, 0), (0, 4), (0, 0))).reshape(128, 128)
    return left, jnp.concatenate([right, rdown, ldown], axis=0)


def unpack(first, rest):
    left = jnp.transpose(first.reshape(2, 4, 16, 8, 16), (0, 1, 3, 2, 4)).reshape(2, HALF, 256)
    right = jnp.transpose(rest[:RD_AT].reshape(2, 2, 2, HALF, 128), (1, 3, 2, 0, 4))
    right = right.reshape(2, HALF, 2, 8, 32)[..., :28].reshape(2, HALF, 448)
    rdown = jnp.transpose(rest[RD_AT:LD_AT].reshape(2, HALF, 128), (1, 0, 2)).reshape(HALF, 256)
    ldown = rest[LD_AT:].reshape(4, 32, 8, 16)[:, :28]
    ldown = jnp.transpose(ldown, (0, 2, 1, 3)).reshape(HALF, 448)
    return left[0], right[0], left[1], right[1], ldown, rdown


def turn_blocks(v):
    whole = v.reshape(-1, 8, 128)
    row = lax.broadcasted_iota(jnp.int32, (1, 8, 128), 1)
    lane = lax.broadcasted_iota(jnp.int32, (1, 8, 128), 2) // RANK
    out = whole
    for s in range(1, 8):
        moved = pltpu.roll(pltpu.roll(whole, s, 1), 128 - RANK * s, 2)
        out = jnp.where((row - lane - s) % 8 == 0, moved, out)
    return out


def spaced(v):
    gap = jnp.zeros((v.shape[0], 4), f32)
    parts = []
    for q in range(8):
        parts += [v[:, 28 * q : 28 * q + 28], gap]
    return jnp.concatenate(parts, axis=1)


def prepare_body(where, *refs):
    shards, (x, y, packed, x_out, y_out), (lg, rg, lu, ru, ld, rd) = refs[:6], refs[6:11], refs[11:17]
    sems, shard_sems = refs[17:]
    half = x_out.shape[0]
    off = pl.multiple_of((1 - where[1]) * half, half)
    loads = [
        pltpu.make_async_copy(shard, ref, shard_sems.at[i])
        for i, (shard, ref) in enumerate(zip(shards, refs[11:17]))
    ]
    copies = [
        pltpu.make_async_copy(x.at[pl.ds(off, half), :], x_out, sems.at[0]),
        pltpu.make_async_copy(y.at[pl.ds(off, half), :], y_out, sems.at[1]),
    ]
    for copy in loads + copies:
        copy.start()
    for copy in loads:
        copy.wait()
    for gu, ref in enumerate([lg, lu]):
        v = ref[...].astype(f32)
        lo, hi = turn_blocks(v[:, :128]), turn_blocks(v[:, 128:])
        for g in range(4):
            both = jnp.concatenate([lo[g], hi[g]], axis=0)
            packed[pl.ds((gu * 4 + g) * 16, 16), :] = both.astype(bf16)
    for gu, ref in enumerate([rg, ru]):
        v = ref[...].astype(f32)
        for al in range(2):
            part = spaced(v[:, al * BHID : (al + 1) * BHID]).astype(bf16)
            for h in range(2):
                at = FIRST + h * 128 + gu * 64 + al * HALF
                packed[pl.ds(at, HALF), :] = part[:, h * 128 : (h + 1) * 128]
    for al in range(2):
        packed[pl.ds(FIRST + RD_AT + al * HALF, HALF), :] = rd[:, pl.ds(al * 128, 128)]
    v = ld[...].astype(f32)
    v = jnp.concatenate([v, jnp.zeros((HALF, 64), f32)], axis=1)
    quarters = [turn_blocks(v[:, q * 128 : (q + 1) * 128]) for q in range(4)]
    for g in range(4):
        part = jnp.concatenate([q[g] for q in quarters], axis=0).astype(bf16)
        packed[pl.ds(FIRST + LD_AT + g * 32, 32), :] = part
    for copy in copies:
        copy.wait()


def finish_body(first, rights, downs, lg, rg, lu, ru, ld, rd):
    def total(pieces, start, height):
        return sum(p[pl.ds(start, height), :].astype(f32) for p in pieces)

    left = total(first, 0, FIRST)
    for gu, ref in enumerate([lg, lu]):
        v = left[gu * 64 : (gu + 1) * 64].reshape(4, 2, 8, 128)
        for h in range(2):
            ref[:, pl.ds(h * 128, 128)] = turn_blocks(v[:, h]).reshape(HALF, 128)
    right = total(rights, 0, RIGHT)
    for gu, ref in enumerate([rg, ru]):
        parts = []
        for al in range(2):
            for q in range(8):
                at = (q // 4) * 128 + gu * 64 + al * HALF
                parts.append(right[at : at + HALF, 32 * (q % 4) : 32 * (q % 4) + 28])
        ref[...] = jnp.concatenate(parts, axis=1)
    down = total(downs, 0, 64)
    for al in range(2):
        rd[:, pl.ds(al * 128, 128)] = down[al * HALF : (al + 1) * HALF]
    v = total(downs, 64, 128).reshape(4, 4, 8, 128)
    parts = [turn_blocks(v[:, q]).reshape(HALF, 128) for q in range(4)]
    ld[...] = jnp.concatenate(parts, axis=1)[:, :448]


def nn(a, b):
    return jnp.dot(a, b, preferred_element_type=f32)


def rounded(v):
    return v.astype(bf16).astype(f32)


def rows(j, height=RANK):
    return pl.ds(pl.multiple_of(j * height, height), height)


def lanes(j, width=BIN):
    return pl.ds(pl.multiple_of(j * width, width), width)


def spread(v, masks):
    return jnp.concatenate([v * mask for mask in masks], axis=0)


def chosen(out, toks):
    slot = lax.broadcasted_iota(jnp.int32, (toks, 128), 1) // RANK
    total = out[:toks]
    for u in range(1, GROUP):
        total = jnp.where(slot == u, out[u * toks : (u + 1) * toks], total)
    return total


def crossed_pair(a, b):
    return jnp.concatenate(
        [jnp.concatenate([a, jnp.zeros_like(b)], axis=1), jnp.concatenate([jnp.zeros_like(a), b], axis=1)], axis=0
    )


def unit_masks():
    slot = lax.broadcasted_iota(jnp.int32, (1, 128), 1) // RANK
    return [jnp.where(slot == u, 1.0, 0.0).astype(bf16) for u in range(GROUP)]


def chunk_of(me, r):
    return me ^ (2 * (r % 4)) ^ (r // 4)


def inner_body(other, where, along, across, x, inner, t_l, xs, sem):
    me, side = where[0], where[1]
    toks = xs.shape[0]
    off = 0 if other else pl.multiple_of(side * toks, toks)
    copy = pltpu.make_async_copy(x.at[pl.ds(off, toks), :], xs, sem)
    copy.start()
    masks = [jnp.concatenate([mask, mask], axis=1) for mask in unit_masks()]
    for r in range(CHUNKS):
        piece = (along, across)[r // 4]
        for gg in range(8):
            t_l[gg, rows(chunk_of(me, r)), :] = piece[r % 4, pl.ds(gg * 16, 16), :]
    copy.wait()

    def step(i, _):
        both = jnp.concatenate([t_l[i], t_l[4 + i]], axis=1)
        total = jnp.zeros((toks, 256), f32)
        for p in range(GROUP // 2):
            w = jnp.concatenate([both * masks[2 * p + h] for h in range(2)], axis=0)
            total += nn(xs[:, lanes(i * GROUP // 2 + p, 256)], w)
        for gu in range(2):
            inner[gu, rows(i, 128), :] = rounded(total[:, gu * 128 : (gu + 1) * 128].T)
        return 0

    lax.fori_loop(0, 4, step, 0)


def by_parity(ref, m):
    return jnp.concatenate(
        [ref[pl.ds(m, 8, stride=2 * NB), :], ref[pl.ds(m + NB, 8, stride=2 * NB), :]], axis=0
    ).astype(bf16)


def middle_body(
    scale, where, order, own_a, own_b, oth_a, oth_b, inner_own, inner_oth, y, y_got, keep, send,
    inner, ret, t_r, n_ld, act_own, act_oth, slope_own, slope_oth,
    ys, sems, r_lo, r_hi, s_rd, n_r, n_rd, t_rd, t_ld, g_out, down, hid_s,
):
    me, side = where[0], where[1]
    toks = ys.shape[1]
    copies = [
        pltpu.make_async_copy(y.at[pl.ds(pl.multiple_of(side * toks, toks), toks), :], ys.at[0], sems.at[0]),
        pltpu.make_async_copy(y_got, ys.at[1], sems.at[1]),
    ]
    for copy in copies:
        copy.start()
    masks = unit_masks()
    s_r = (r_lo, r_hi)
    for gu in range(2):
        for b, part in enumerate([inner_own, inner_oth]):
            inner[rows(gu * 2 + (side ^ b), 512), :] = part[gu]

    for b, pieces in enumerate([(own_a, own_b), (oth_a, oth_b)]):
        blk = side ^ b
        for r in range(CHUNKS):
            d = chunk_of(me, r)
            ref, at = pieces[r // 4], r % 4
            for gu in range(2):
                for al in range(2):
                    row = pl.multiple_of((2 * d + al) * 128 + gu * NB + blk * HALF, HALF)
                    for half in range(2):
                        src = FIRST + half * 128 + gu * 64 + al * HALF
                        s_r[half][pl.ds(row, HALF), :] = ref[at, pl.ds(src, HALF), :].astype(f32)
            for al in range(2):
                row = pl.multiple_of((2 * d + al) * NB + blk * HALF, HALF)
                s_rd[pl.ds(row, HALF), :] = ref[at, pl.ds(FIRST + RD_AT + al * HALF, HALF), :].astype(f32)
            for g in range(4):
                t_ld[blk * 4 + g, rows(d, 32), :] = ref[at, pl.ds(FIRST + LD_AT + g * 32, 32), :]

    def stacked(ref, start, stride, g):
        return jnp.concatenate(
            [ref[pl.ds(start + g * GROUP + u, RANK, stride=stride), :] for u in range(GROUP)], axis=0
        )

    def turn(g, _):
        for gu in range(2):
            for h in range(2):
                flat = stacked(s_r[h], gu * NB, 128, g)
                n_r[gu, g, :, pl.ds(h * 128, 128)] = flat.astype(bf16)
                t_r[gu, g, pl.ds(h * 128, 128), :] = flat.T.astype(bf16)
        for h in range(2):
            part = t_ld[g, pl.ds(h * 128, 128), :].astype(f32).T
            n_ld[g, :, pl.ds(h * 128, 128)] = part.astype(bf16)
        flat = stacked(s_rd, 0, NB, g)
        n_rd[g] = flat.astype(bf16)
        t_rd[g] = flat.T.astype(bf16)
        return 0

    lax.fori_loop(0, GROUPS, turn, 0)

    def blocks(g):
        return [(u, g * GROUP + u) for u in range(GROUP)]

    def second(i, _, b):
        g = (side ^ b) * 4 + i
        act_s, slope_s = ((act_own, slope_own), (act_oth, slope_oth))[b]
        turned = []
        for gu in range(2):
            mixed = [inner[pl.ds(gu * 1024 + order[k], RANK, stride=NB), :] for u, k in blocks(g)]
            turned.append(jnp.concatenate(mixed, axis=0).T.astype(bf16))
        span = pl.ds(pl.multiple_of(i * GROUP, GROUP), GROUP)
        act_s[span] = nn(spread(turned[0], masks), n_r[0, g]).reshape(GROUP, toks, WIDE)
        slope_s[span] = nn(spread(turned[1], masks), n_r[1, g]).reshape(GROUP, toks, WIDE)
        for u, k in blocks(g):
            local = i * GROUP + u
            gate, upper = act_s[local], slope_s[local]
            sig = 0.5 * jnp.tanh(0.5 * gate) + 0.5
            act = gate * sig
            act_s[local] = act
            slope_s[local] = upper * (sig + act * (1.0 - sig))
            hid_s[k] = (act * upper).astype(bf16)
        hidden = hid_s[pl.ds(pl.multiple_of(g * GROUP, GROUP), GROUP)].reshape(GROUP * toks, WIDE)
        total = chosen(nn(hidden, t_ld[g]), toks)
        down[rows(g, 128), :] = rounded(total.T)
        return 0

    for b in range(2):
        lax.fori_loop(0, 4, functools.partial(second, b=b), 0)

    def put(b, base, value):
        for al in range(2):
            g_out[b, pl.ds(base + al * HALF, 8, stride=DOWN), :] = value[al * 8 : (al + 1) * 8]

    for b in range(2):
        copies[b].wait()

        def third(i, _, b=b):
            g = (side ^ b) * 4 + i
            dms = [down[pl.ds(order[k], RANK, stride=NB), :] for u, k in blocks(g)]
            turned = jnp.concatenate(dms, axis=0).T.astype(bf16)
            student = nn(spread(turned, masks), n_rd[g])
            deltas = []
            for u, k in blocks(g):
                target = ys[b, :, lanes(i * GROUP + u)].astype(f32)
                part = student[u * toks : (u + 1) * toks]
                deltas.append(((part - target) * scale).astype(bf16))
            total = chosen(nn(jnp.concatenate(deltas, axis=0), t_rd[g]), toks)
            parity = [by_parity(down, order[k]) for u, k in blocks(g)]
            for q in range(2):
                d = deltas[4 * q : 4 * q + 4]
                m = parity[4 * q : 4 * q + 4]
                grads = nn(
                    crossed_pair(jnp.concatenate(m[:2], axis=0), jnp.concatenate(m[2:], axis=0)),
                    jnp.concatenate([jnp.concatenate(d[:2], axis=1), jnp.concatenate(d[2:], axis=1)], axis=0),
                )
                for e in range(4):
                    part = grads[e * RANK : (e + 1) * RANK, (e % 2) * 128 : (e % 2 + 1) * 128]
                    put(b, i * GROUP + 4 * q + e, part)
            total = rounded(total.T)
            for u, k in blocks(g):
                ret[pl.ds(order[k], RANK, stride=NB), :] = total[u * RANK : (u + 1) * RANK]
            return 0

        lax.fori_loop(0, 4, third, 0)

    def inward(i, _, b):
        g = (side ^ b) * 4 + i
        returned = ret[rows(g, 128), :].astype(bf16)
        grads = []
        for p in range(GROUP // 2):
            pair = [returned[u * RANK : (u + 1) * RANK] for u in (2 * p, 2 * p + 1)]
            both = hid_s[pl.ds(g * GROUP + 2 * p, 2)].reshape(2 * toks, WIDE)
            grads.append(nn(crossed_pair(*pair), both))
        grads = jnp.concatenate(grads, axis=0)
        for h in range(2):
            part = grads[:, h * 128 : (h + 1) * 128].T
            for q in range(4):
                at = (h * 4 + q) * DOWN + 64 + i * 32
                g_out[b, pl.ds(pl.multiple_of(at, 32), 32), :] = part[q * 32 : (q + 1) * 32]
        return 0

    for b in range(2):
        lax.fori_loop(0, 4, functools.partial(inward, b=b), 0)

    for b, out in enumerate([keep, send]):
        for r in range(CHUNKS):
            out[r] = g_out[b, rows(chunk_of(me, r), DOWN), :].astype(bf16)


def right_body(b, where, order, inner, ret, t_r, n_ld, act_s, slope_s, *refs):
    if b == 0:
        before, grads_out, back, g_out = refs
        back[...] = before[...]
    else:
        grads_out, back, g_out = refs
    me, side = where[0], where[1]
    toks = inner.shape[1]
    masks = unit_masks()

    def step(i, _):
        g = (side ^ b) * 4 + i
        blocks = [(u, g * GROUP + u) for u in range(GROUP)]
        turned = ret[rows(g, 128), :].T.astype(bf16)
        dhidden = nn(spread(turned, masks), n_ld[g])
        sent = ([], [])
        for u, j in blocks:
            local, part = i * GROUP + u, dhidden[u * toks : (u + 1) * toks]
            sent[0].append((part * slope_s[local]).astype(bf16))
            sent[1].append((part * act_s[local]).astype(bf16))
        for gu in range(2):
            total = rounded(chosen(nn(jnp.concatenate(sent[gu], axis=0), t_r[gu, g]), toks).T)
            for u, j in blocks:
                back[pl.ds(gu * 1024 + order[j], RANK, stride=NB), :] = total[u * RANK : (u + 1) * RANK]
        for u, j in blocks:
            mixed = [by_parity(inner, gu * 1024 + order[j]) for gu in range(2)]
            grad = nn(crossed_pair(*mixed), jnp.concatenate([sent[0][u], sent[1][u]], axis=0))
            for gu in range(2):
                for h in range(2):
                    base = h * 128 + gu * 64 + i * GROUP + u
                    for al in range(2):
                        g_out[pl.ds(base + al * HALF, 8, stride=RIGHT), :] = grad[
                            gu * RANK + al * 8 : gu * RANK + (al + 1) * 8, h * 128 : (h + 1) * 128
                        ]
        return 0

    lax.fori_loop(0, 4, step, 0)
    for r in range(CHUNKS):
        grads_out[r] = g_out[rows(chunk_of(me, r), RIGHT), :].astype(bf16)


def left_body(where, back, x, x_got, keep, send, turned, xs, sems):
    me, side = where[0], where[1]
    toks = xs.shape[1]
    copies = [
        pltpu.make_async_copy(x.at[pl.ds(pl.multiple_of(side * toks, toks), toks), :], xs.at[0], sems.at[0]),
        pltpu.make_async_copy(x_got, xs.at[1], sems.at[1]),
    ]
    for copy in copies:
        copy.start()
    for b, out in enumerate([keep, send]):
        copies[b].wait()

        def step(i, _, b=b):
            parts = ([], [])
            for q in range(2):
                both = []
                for u in range(4 * q, 4 * q + 4):
                    j = ((side ^ b) * 4 + i) * GROUP + u
                    both += [back[rows(j), :], back[rows(j + NB), :]]
                both = jnp.concatenate(both, axis=0).astype(bf16)
                at = i * 4 + 2 * q
                x4 = jnp.concatenate([xs[b, :, lanes(at, 256)], xs[b, :, lanes(at + 1, 256)]], axis=0)
                grads = nn(crossed_pair(both[:64], both[64:]), x4)
                for e in range(4):
                    for gu in range(2):
                        top = (e * 2 + gu) * RANK
                        parts[gu].append(grads[top : top + RANK, (e % 2) * 128 : (e % 2 + 1) * 128])
            for gu in range(2):
                turned[rows(gu * 4 + i, 128), :] = jnp.concatenate(parts[gu], axis=0).T.astype(bf16)
            return 0

        lax.fori_loop(0, 4, step, 0)
        for r in range(CHUNKS):
            d = chunk_of(me, r)
            for gg in range(8):
                at = pl.multiple_of(gg * 128 + d * 16, 16)
                out[r, pl.ds(gg * 16, 16), :] = turned[pl.ds(at, 16), :]


VMEM = pl.BlockSpec(memory_space=pltpu.VMEM)
SMEM = pl.BlockSpec(memory_space=pltpu.SMEM)


ANY = pl.BlockSpec(memory_space=pl.ANY)
HBM = pl.BlockSpec(memory_space=pltpu.HBM)
VMEM_MIDDLE = 20 * 2**20
VMEM_RIGHT = 10 * 2**20


def prepare_call(where, factors, x, y):
    sent = jax.ShapeDtypeStruct((x.shape[0] // 2, x.shape[1]), bf16)
    return pl.pallas_call(
        prepare_body,
        out_shape=(jax.ShapeDtypeStruct((FIRST + REST, 128), bf16), sent, sent),
        in_specs=[SMEM] + [HBM] * 8,
        out_specs=(VMEM, VMEM, VMEM),
        scratch_shapes=[pltpu.VMEM(v.shape, bf16) for v in factors]
        + [pltpu.SemaphoreType.DMA((2,)), pltpu.SemaphoreType.DMA((6,))],
        compiler_params=pltpu.CompilerParams(vmem_limit_bytes=60 * 2**20),
    )(where, *factors, x, y)


def finish_call(first, rights, downs):
    cut, count = len(first), len(first) + len(rights) + len(downs)
    turn = cut + len(rights)
    shapes = [256, 448, 256, 448, 448, 256]
    return pl.pallas_call(
        lambda *refs: finish_body(refs[:cut], refs[cut:turn], refs[turn:count], *refs[count:]),
        out_shape=tuple(jax.ShapeDtypeStruct((HALF, c), f32) for c in shapes),
        in_specs=[VMEM] * count,
        out_specs=(VMEM,) * 6,
        compiler_params=pltpu.CompilerParams(vmem_limit_bytes=16 * 2**20),
    )(*first, *rights, *downs)


def inner_call(other, where, along, across, x, toks):
    front = pl.BlockSpec((4, FIRST, 128), lambda i: (0, 0, 0))
    return pl.pallas_call(
        functools.partial(inner_body, other),
        grid=(1,),
        out_shape=jax.ShapeDtypeStruct((2, NB * RANK // 2, toks), f32),
        in_specs=[SMEM, front, front, ANY],
        out_specs=VMEM,
        scratch_shapes=[
            pltpu.VMEM((8, BIN, 128), bf16),
            pltpu.VMEM((toks, x.shape[1]), bf16),
            pltpu.SemaphoreType.DMA,
        ],
        compiler_params=pltpu.CompilerParams(vmem_limit_bytes=16 * 2**20),
        cost_estimate=pl.CostEstimate(flops=10**9, bytes_accessed=10**7, transcendentals=0),
    )(where, along, across, x)


def middle_call(scale, where, order, pieces, inner, y, y_got):
    toks = y_got.shape[0]
    down = jax.ShapeDtypeStruct((CHUNKS, DOWN, 128), bf16)
    kept = jax.ShapeDtypeStruct((HALF, toks, WIDE), f32)
    return pl.pallas_call(
        functools.partial(middle_body, scale),
        out_shape=(
            down,
            down,
            jax.ShapeDtypeStruct((2 * NB * RANK, toks), f32),
            jax.ShapeDtypeStruct((NB * RANK, toks), f32),
            jax.ShapeDtypeStruct((2, GROUPS, WIDE, 128), bf16),
            jax.ShapeDtypeStruct((GROUPS, 128, WIDE), bf16),
            kept,
            kept,
            kept,
            kept,
        ),
        in_specs=[SMEM, SMEM] + [VMEM] * 6 + [ANY] * 2,
        out_specs=(VMEM,) * 10,
        scratch_shapes=[
            pltpu.VMEM((2,) + y_got.shape, bf16),
            pltpu.SemaphoreType.DMA((2,)),
            pltpu.VMEM((RANK * 128, 128), f32),
            pltpu.VMEM((RANK * 128, 128), f32),
            pltpu.VMEM((RANK * NB, 128), f32),
            pltpu.VMEM((2, GROUPS, 128, WIDE), bf16),
            pltpu.VMEM((GROUPS, 128, BIN), bf16),
            pltpu.VMEM((GROUPS, BIN, 128), bf16),
            pltpu.VMEM((GROUPS, WIDE, 128), bf16),
            pltpu.VMEM((2, CHUNKS * DOWN, 128), f32),
            pltpu.VMEM((NB * RANK, toks), f32),
            pltpu.VMEM((NB, toks, WIDE), bf16),
        ],
        compiler_params=pltpu.CompilerParams(vmem_limit_bytes=VMEM_MIDDLE),
        cost_estimate=pl.CostEstimate(flops=5 * 10**9, bytes_accessed=4 * 10**7, transcendentals=0),
    )(where, order, *pieces, *inner, y, y_got)


def right_call(b, where, order, *arrays):
    toks = arrays[0].shape[1]
    return pl.pallas_call(
        functools.partial(right_body, b),
        out_shape=(
            jax.ShapeDtypeStruct((CHUNKS, RIGHT, 128), bf16),
            jax.ShapeDtypeStruct((2 * NB * RANK, toks), f32),
        ),
        in_specs=[SMEM, SMEM] + [VMEM] * len(arrays),
        out_specs=(VMEM, VMEM),
        scratch_shapes=[pltpu.VMEM((CHUNKS * RIGHT, 128), f32)],
        compiler_params=pltpu.CompilerParams(vmem_limit_bytes=VMEM_RIGHT),
        cost_estimate=pl.CostEstimate(flops=5 * 10**9, bytes_accessed=2 * 10**7, transcendentals=0),
    )(where, order, *arrays)


def left_call(where, back, x, x_got):
    grads = jax.ShapeDtypeStruct((CHUNKS, FIRST, 128), bf16)
    return pl.pallas_call(
        left_body,
        out_shape=(grads, grads),
        in_specs=[SMEM, VMEM, ANY, ANY],
        out_specs=(VMEM, VMEM),
        scratch_shapes=[
            pltpu.VMEM((8 * 128, 128), bf16),
            pltpu.VMEM((2,) + x_got.shape, bf16),
            pltpu.SemaphoreType.DMA((2,)),
        ],
        compiler_params=pltpu.CompilerParams(vmem_limit_bytes=16 * 2**20),
        cost_estimate=pl.CostEstimate(flops=10**9, bytes_accessed=10**7, transcendentals=0),
    )(where, back, x, x_got)


def swap(v, axis, bit, size):
    return lax.ppermute(v, axis, [(i, i ^ bit) for i in range(size)])


def sibling(v):
    return swap(v, "blk", 1, 2)


def gathered(mine, n):
    along = [mine] + [swap(mine, "dp", 2 * s, n) for s in range(1, 4)]
    across = [swap(v, "dp", 1, n) for v in along]
    along, across = jnp.stack(along), jnp.stack(across)
    return along, across, sibling(along), sibling(across)


def add(a, b):
    return (a.astype(f32) + b.astype(f32)).astype(bf16)


def tie(value, *others):
    return lax.optimization_barrier((value,) + others)[0]


def along_z(line, n):
    return [swap(line[s], "dp", 2 * s, n) for s in range(1, 4)]


def by_z_then_x(keep, got, n):
    both = add(keep, got)
    both = both.reshape((2, 4) + both.shape[1:])
    pair = both[:, 0].astype(f32)
    for s in range(1, 4):
        pair = pair + swap(both[:, s], "dp", 2 * s, n).astype(f32)
    pair = pair.astype(bf16)
    return [pair[0], swap(pair[1], "dp", 1, n)]


def on_device(activations, teacher_out, block_order, *factors):
    n = lax.axis_size("dp")
    me = lax.axis_index("dp")
    side = lax.axis_index("blk")
    toks = activations.shape[0] // 2
    scale = float(activations.shape[0] * n) ** (-0.5)
    direct = n == CHUNKS
    if direct:
        where = jnp.stack([me, side]).astype(jnp.int32)
        mine, x_sent, y_sent = prepare_call(where, factors, activations, teacher_out)
        pieces = gathered(mine, n)
    else:
        where = jnp.stack([jnp.zeros_like(side), side]).astype(jnp.int32)
        whole = [lax.all_gather(v, "dp", axis=1, tiled=True) for v in factors]
        cut = [jnp.moveaxis(v.reshape(HALF, CHUNKS, -1), 1, 0) for v in whole]
        packed = jnp.concatenate(jax.vmap(pack)(*cut), axis=1)
        pieces = (packed[0::2], packed[1::2], sibling(packed[0::2]), sibling(packed[1::2]))
        x_sent, y_sent = [
            lax.dynamic_slice_in_dim(v, (1 - side) * toks, toks, 0) for v in (activations, teacher_out)
        ]
    x_got, y_got = sibling(x_sent), sibling(y_sent)
    inner = (
        inner_call(False, where, pieces[0], pieces[1], activations, toks),
        inner_call(True, where, pieces[2], pieces[3], x_got, toks),
    )
    keep, send, *state = middle_call(scale, where, block_order, pieces, inner, teacher_out, y_got)
    shared, (act_own, act_oth, slope_own, slope_oth) = state[:4], state[4:]
    got = sibling(send)
    right_send, back = right_call(1, where, block_order, *shared, act_oth, slope_oth)
    right_got = sibling(right_send)
    if direct:
        away = add(keep[4:], got[4:])
        here = add(keep[:4], got[:4])
        crossed = swap(away, "dp", 1, n)
        back = tie(back, away, here)
    right_keep, back = right_call(0, where, block_order, *shared, act_own, slope_own, back)
    if direct:
        right_away = add(right_keep[4:], right_got[4:])
        right_here = add(right_keep[:4], right_got[:4])
        right_crossed = swap(right_away, "dp", 1, n)
        line = add(here, crossed)
        down = [line[0]] + along_z(line, n)
        back = tie(back, right_away, line)
    left_keep, left_send = left_call(where, back, activations, x_got)
    left_got = sibling(left_send)
    if direct:
        right_line = add(right_here, right_crossed)
        right = [right_line[0]] + along_z(right_line, n)
        left = by_z_then_x(left_keep, left_got, n)
        return finish_call(left, right, down)
    rest = (jnp.concatenate([right_keep, keep], axis=1), jnp.concatenate([right_got, got], axis=1))
    sums = []
    rest = [jnp.concatenate(v, axis=1) for v in ((right_keep, keep), (right_send, send))]
    for own, away in ((left_keep, left_got), rest):
        total = own.astype(f32) + away.astype(f32)
        sums.append(jnp.stack([total[:4], total[4:]], axis=1).reshape(total.shape))
    parts = jax.vmap(unpack)(*sums)
    parts = [jnp.moveaxis(v, 0, 1).reshape(HALF, -1) for v in parts]
    return tuple(lax.psum_scatter(v, "dp", scatter_dimension=1, tiled=True) for v in parts)


def solution(mesh):
    tokens = P(("group", "dp"), "blk")
    factor = P("blk", "dp")
    grad = P(("group", "blk"), "dp")
    return jax.shard_map(
        on_device,
        mesh=mesh,
        in_specs=(tokens, tokens, P()) + (factor,) * 6,
        out_specs=(grad,) * 6,
        check_vma=False,
    )
```

```python
import functools

import jax
import jax.numpy as jnp
from jax import lax
from jax.experimental import pallas as pl
from jax.experimental.pallas import tpu as pltpu
from jax.sharding import PartitionSpec as P

NB = 64
HALF = 32
RANK = 16
BIN = 128
BHID = 224
WIDE = 256
CHUNKS = 8
GROUP = 8
GROUPS = NB // GROUP
f32 = jnp.float32
bf16 = jnp.bfloat16

STEPS = (0, 2, 1, 3)
FIRST = 128
REST = 448
RD_AT = 256
LD_AT = 320
RIGHT = 256
DOWN = 192


def pack(lg, rg, lu, ru, ld, rd):
    left = jnp.stack([lg, lu]).reshape(2, 4, 8, 16, 16)
    left = jnp.transpose(left, (0, 1, 3, 2, 4)).reshape(FIRST, 128)
    right = jnp.stack([rg, ru]).reshape(2, HALF, 2, 8, 28)
    right = jnp.pad(right, ((0, 0),) * 4 + ((0, 4),)).reshape(2, HALF, 2, 2, 128)
    right = jnp.transpose(right, (3, 0, 2, 1, 4)).reshape(256, 128)
    rdown = jnp.transpose(rd.reshape(HALF, 2, 128), (1, 0, 2)).reshape(64, 128)
    ldown = jnp.transpose(ld.reshape(4, 8, 28, 16), (0, 2, 1, 3)).reshape(4, 28, 128)
    ldown = jnp.pad(ldown, ((0, 0), (0, 4), (0, 0))).reshape(128, 128)
    return left, jnp.concatenate([right, rdown, ldown], axis=0)


def unpack(first, rest):
    left = jnp.transpose(first.reshape(2, 4, 16, 8, 16), (0, 1, 3, 2, 4)).reshape(2, HALF, 256)
    right = jnp.transpose(rest[:RD_AT].reshape(2, 2, 2, HALF, 128), (1, 3, 2, 0, 4))
    right = right.reshape(2, HALF, 2, 8, 32)[..., :28].reshape(2, HALF, 448)
    rdown = jnp.transpose(rest[RD_AT:LD_AT].reshape(2, HALF, 128), (1, 0, 2)).reshape(HALF, 256)
    ldown = rest[LD_AT:].reshape(4, 32, 8, 16)[:, :28]
    ldown = jnp.transpose(ldown, (0, 2, 1, 3)).reshape(HALF, 448)
    return left[0], right[0], left[1], right[1], ldown, rdown


def turn_blocks(v):
    whole = v.reshape(-1, 8, 128)
    row = lax.broadcasted_iota(jnp.int32, (1, 8, 128), 1)
    lane = lax.broadcasted_iota(jnp.int32, (1, 8, 128), 2) // RANK
    out = whole
    for s in range(1, 8):
        moved = pltpu.roll(pltpu.roll(whole, s, 1), 128 - RANK * s, 2)
        out = jnp.where((row - lane - s) % 8 == 0, moved, out)
    return out


def spaced(v):
    gap = jnp.zeros((v.shape[0], 4), f32)
    parts = []
    for q in range(8):
        parts += [v[:, 28 * q : 28 * q + 28], gap]
    return jnp.concatenate(parts, axis=1)


def prepare_body(*refs):
    shards, packed, (lg, rg, lu, ru, ld, rd), sems = refs[:6], refs[6], refs[7:13], refs[13]
    loads = [
        pltpu.make_async_copy(shard, ref, sems.at[i]) for i, (shard, ref) in enumerate(zip(shards, refs[7:13]))
    ]
    for copy in loads:
        copy.start()
    for copy in loads:
        copy.wait()
    for gu, ref in enumerate([lg, lu]):
        v = ref[...].astype(f32)
        lo, hi = turn_blocks(v[:, :128]), turn_blocks(v[:, 128:])
        for g in range(4):
            both = jnp.concatenate([lo[g], hi[g]], axis=0)
            packed[pl.ds((gu * 4 + g) * 16, 16), :] = both.astype(bf16)
    for gu, ref in enumerate([rg, ru]):
        v = ref[...].astype(f32)
        for al in range(2):
            part = spaced(v[:, al * BHID : (al + 1) * BHID]).astype(bf16)
            for h in range(2):
                at = FIRST + h * 128 + gu * 64 + al * HALF
                packed[pl.ds(at, HALF), :] = part[:, h * 128 : (h + 1) * 128]
    for al in range(2):
        packed[pl.ds(FIRST + RD_AT + al * HALF, HALF), :] = rd[:, pl.ds(al * 128, 128)]
    v = ld[...].astype(f32)
    v = jnp.concatenate([v, jnp.zeros((HALF, 64), f32)], axis=1)
    quarters = [turn_blocks(v[:, q * 128 : (q + 1) * 128]) for q in range(4)]
    for g in range(4):
        part = jnp.concatenate([q[g] for q in quarters], axis=0).astype(bf16)
        packed[pl.ds(FIRST + LD_AT + g * 32, 32), :] = part


def finish_body(first, rights, downs, lg, rg, lu, ru, ld, rd):
    def total(pieces, start, height):
        return sum(p[pl.ds(start, height), :].astype(f32) for p in pieces)

    left = total(first, 0, FIRST)
    for gu, ref in enumerate([lg, lu]):
        v = left[gu * 64 : (gu + 1) * 64].reshape(4, 2, 8, 128)
        for h in range(2):
            ref[:, pl.ds(h * 128, 128)] = turn_blocks(v[:, h]).reshape(HALF, 128)
    right = total(rights, 0, RIGHT)
    for gu, ref in enumerate([rg, ru]):
        parts = []
        for al in range(2):
            for q in range(8):
                at = (q // 4) * 128 + gu * 64 + al * HALF
                parts.append(right[at : at + HALF, 32 * (q % 4) : 32 * (q % 4) + 28])
        ref[...] = jnp.concatenate(parts, axis=1)
    down = total(downs, 0, 64)
    for al in range(2):
        rd[:, pl.ds(al * 128, 128)] = down[al * HALF : (al + 1) * HALF]
    v = total(downs, 64, 128).reshape(4, 4, 8, 128)
    parts = [turn_blocks(v[:, q]).reshape(HALF, 128) for q in range(4)]
    ld[...] = jnp.concatenate(parts, axis=1)[:, :448]


def nn(a, b):
    return jnp.dot(a, b, preferred_element_type=f32)


def rounded(v):
    return v.astype(bf16).astype(f32)


def rows(j, height=RANK):
    return pl.ds(pl.multiple_of(j * height, height), height)


def lanes(j, width=BIN):
    return pl.ds(pl.multiple_of(j * width, width), width)


def spread(v, masks):
    return jnp.concatenate([v * mask for mask in masks], axis=0)


def chosen(out, toks):
    slot = lax.broadcasted_iota(jnp.int32, (toks, 128), 1) // RANK
    total = out[:toks]
    for u in range(1, GROUP):
        total = jnp.where(slot == u, out[u * toks : (u + 1) * toks], total)
    return total


def crossed_pair(a, b):
    return jnp.concatenate(
        [jnp.concatenate([a, jnp.zeros_like(b)], axis=1), jnp.concatenate([jnp.zeros_like(a), b], axis=1)], axis=0
    )


def unit_masks():
    slot = lax.broadcasted_iota(jnp.int32, (1, 128), 1) // RANK
    return [jnp.where(slot == u, 1.0, 0.0).astype(bf16) for u in range(GROUP)]


def tokens_at(ref, side, toks):
    return pl.ds(0, toks) if ref.shape[0] == toks else pl.ds(pl.multiple_of(side * toks, toks), toks)


def chunk_of(me, r):
    return me ^ (2 * STEPS[r % 4]) ^ (r // 4)


def inner_body(where, along, across, x, inner, t_l):
    me = where[0]
    toks = inner.shape[2]
    at = tokens_at(x, where[1], toks)
    masks = [jnp.concatenate([mask, mask], axis=1) for mask in unit_masks()]
    for r in range(CHUNKS):
        piece = (along, across)[r // 4]
        for gg in range(8):
            t_l[gg, rows(chunk_of(me, r)), :] = piece[r % 4, pl.ds(gg * 16, 16), :]

    def step(i, _):
        both = jnp.concatenate([t_l[i], t_l[4 + i]], axis=1)
        total = jnp.zeros((toks, 256), f32)
        for p in range(GROUP // 2):
            w = jnp.concatenate([both * masks[2 * p + h] for h in range(2)], axis=0)
            total += nn(x[at, lanes(i * GROUP // 2 + p, 256)], w)
        for gu in range(2):
            inner[gu, rows(i, 128), :] = rounded(total[:, gu * 128 : (gu + 1) * 128].T)
        return 0

    lax.fori_loop(0, 4, step, 0)


def by_parity(ref, m):
    return jnp.concatenate(
        [ref[pl.ds(m, 8, stride=2 * NB), :], ref[pl.ds(m + NB, 8, stride=2 * NB), :]], axis=0
    ).astype(bf16)


def middle_body(
    scale, where, order, own_a, own_b, oth_a, oth_b, inner_own, inner_oth, y, y_got, keep, send,
    inner, ret, t_r, n_ld, act_own, act_oth, slope_own, slope_oth,
    r_lo, r_hi, s_rd, n_r, n_rd, t_rd, t_ld, g_out, down, hid_s,
):
    me, side = where[0], where[1]
    toks = inner.shape[1]
    ats = [tokens_at(v, side, toks) for v in (y, y_got)]
    masks = unit_masks()
    s_r = (r_lo, r_hi)
    for gu in range(2):
        for b, part in enumerate([inner_own, inner_oth]):
            inner[rows(gu * 2 + (side ^ b), 512), :] = part[gu]

    for b, pieces in enumerate([(own_a, own_b), (oth_a, oth_b)]):
        blk = side ^ b
        for r in range(CHUNKS):
            d = chunk_of(me, r)
            ref, at = pieces[r // 4], r % 4
            for gu in range(2):
                for al in range(2):
                    row = pl.multiple_of((2 * d + al) * 128 + gu * NB + blk * HALF, HALF)
                    for half in range(2):
                        src = FIRST + half * 128 + gu * 64 + al * HALF
                        s_r[half][pl.ds(row, HALF), :] = ref[at, pl.ds(src, HALF), :].astype(f32)
            for al in range(2):
                row = pl.multiple_of((2 * d + al) * NB + blk * HALF, HALF)
                s_rd[pl.ds(row, HALF), :] = ref[at, pl.ds(FIRST + RD_AT + al * HALF, HALF), :].astype(f32)
            for g in range(4):
                t_ld[blk * 4 + g, rows(d, 32), :] = ref[at, pl.ds(FIRST + LD_AT + g * 32, 32), :]

    def stacked(ref, start, stride, g):
        return jnp.concatenate(
            [ref[pl.ds(start + g * GROUP + u, RANK, stride=stride), :] for u in range(GROUP)], axis=0
        )

    def turn(g, _):
        for gu in range(2):
            for h in range(2):
                flat = stacked(s_r[h], gu * NB, 128, g)
                n_r[gu, g, :, pl.ds(h * 128, 128)] = flat.astype(bf16)
                t_r[gu, g, pl.ds(h * 128, 128), :] = flat.T.astype(bf16)
        for h in range(2):
            part = t_ld[g, pl.ds(h * 128, 128), :].astype(f32).T
            n_ld[g, :, pl.ds(h * 128, 128)] = part.astype(bf16)
        flat = stacked(s_rd, 0, NB, g)
        n_rd[g] = flat.astype(bf16)
        t_rd[g] = flat.T.astype(bf16)
        return 0

    lax.fori_loop(0, GROUPS, turn, 0)

    def blocks(g):
        return [(u, g * GROUP + u) for u in range(GROUP)]

    def second(i, _, b):
        g = (side ^ b) * 4 + i
        act_s, slope_s = ((act_own, slope_own), (act_oth, slope_oth))[b]
        turned = []
        for gu in range(2):
            mixed = [inner[pl.ds(gu * 1024 + order[k], RANK, stride=NB), :] for u, k in blocks(g)]
            turned.append(jnp.concatenate(mixed, axis=0).T.astype(bf16))
        span = pl.ds(pl.multiple_of(i * GROUP, GROUP), GROUP)
        act_s[span] = nn(spread(turned[0], masks), n_r[0, g]).reshape(GROUP, toks, WIDE)
        slope_s[span] = nn(spread(turned[1], masks), n_r[1, g]).reshape(GROUP, toks, WIDE)
        for u, k in blocks(g):
            local = i * GROUP + u
            gate, upper = act_s[local], slope_s[local]
            sig = 0.5 * jnp.tanh(0.5 * gate) + 0.5
            act = gate * sig
            act_s[local] = act
            slope_s[local] = upper * (sig + act * (1.0 - sig))
            hid_s[k] = (act * upper).astype(bf16)
        hidden = hid_s[pl.ds(pl.multiple_of(g * GROUP, GROUP), GROUP)].reshape(GROUP * toks, WIDE)
        total = chosen(nn(hidden, t_ld[g]), toks)
        down[rows(g, 128), :] = rounded(total.T)
        return 0

    for b in range(2):
        lax.fori_loop(0, 4, functools.partial(second, b=b), 0)

    def put(b, base, value):
        for al in range(2):
            g_out[b, pl.ds(base + al * HALF, 8, stride=DOWN), :] = value[al * 8 : (al + 1) * 8]

    for b in range(2):

        def third(i, _, b=b):
            g = (side ^ b) * 4 + i
            dms = [down[pl.ds(order[k], RANK, stride=NB), :] for u, k in blocks(g)]
            turned = jnp.concatenate(dms, axis=0).T.astype(bf16)
            student = nn(spread(turned, masks), n_rd[g])
            deltas = []
            for u, k in blocks(g):
                target = (y, y_got)[b][ats[b], lanes(i * GROUP + u)].astype(f32)
                part = student[u * toks : (u + 1) * toks]
                deltas.append(((part - target) * scale).astype(bf16))
            total = chosen(nn(jnp.concatenate(deltas, axis=0), t_rd[g]), toks)
            parity = [by_parity(down, order[k]) for u, k in blocks(g)]
            for q in range(2):
                d = deltas[4 * q : 4 * q + 4]
                m = parity[4 * q : 4 * q + 4]
                grads = nn(
                    crossed_pair(jnp.concatenate(m[:2], axis=0), jnp.concatenate(m[2:], axis=0)),
                    jnp.concatenate([jnp.concatenate(d[:2], axis=1), jnp.concatenate(d[2:], axis=1)], axis=0),
                )
                for e in range(4):
                    part = grads[e * RANK : (e + 1) * RANK, (e % 2) * 128 : (e % 2 + 1) * 128]
                    put(b, i * GROUP + 4 * q + e, part)
            total = rounded(total.T)
            for u, k in blocks(g):
                ret[pl.ds(order[k], RANK, stride=NB), :] = total[u * RANK : (u + 1) * RANK]
            return 0

        lax.fori_loop(0, 4, third, 0)

    def inward(i, _, b):
        g = (side ^ b) * 4 + i
        returned = ret[rows(g, 128), :].astype(bf16)
        grads = []
        for p in range(GROUP // 2):
            pair = [returned[u * RANK : (u + 1) * RANK] for u in (2 * p, 2 * p + 1)]
            both = hid_s[pl.ds(g * GROUP + 2 * p, 2)].reshape(2 * toks, WIDE)
            grads.append(nn(crossed_pair(*pair), both))
        grads = jnp.concatenate(grads, axis=0)
        for h in range(2):
            part = grads[:, h * 128 : (h + 1) * 128].T
            for q in range(4):
                at = (h * 4 + q) * DOWN + 64 + i * 32
                g_out[b, pl.ds(pl.multiple_of(at, 32), 32), :] = part[q * 32 : (q + 1) * 32]
        return 0

    for b in range(2):
        lax.fori_loop(0, 4, functools.partial(inward, b=b), 0)

    for b, out in enumerate([keep, send]):
        for r in range(CHUNKS):
            out[r] = g_out[b, rows(chunk_of(me, r), DOWN), :].astype(bf16)


def right_body(b, where, order, inner, ret, t_r, n_ld, act_s, slope_s, *refs):
    if b == 0:
        before, grads_out, back, g_out = refs
        back[...] = before[...]
    else:
        grads_out, back, g_out = refs
    me, side = where[0], where[1]
    toks = inner.shape[1]
    masks = unit_masks()

    def step(i, _):
        g = (side ^ b) * 4 + i
        blocks = [(u, g * GROUP + u) for u in range(GROUP)]
        turned = ret[rows(g, 128), :].T.astype(bf16)
        dhidden = nn(spread(turned, masks), n_ld[g])
        sent = ([], [])
        for u, j in blocks:
            local, part = i * GROUP + u, dhidden[u * toks : (u + 1) * toks]
            sent[0].append((part * slope_s[local]).astype(bf16))
            sent[1].append((part * act_s[local]).astype(bf16))
        for gu in range(2):
            total = rounded(chosen(nn(jnp.concatenate(sent[gu], axis=0), t_r[gu, g]), toks).T)
            for u, j in blocks:
                back[pl.ds(gu * 1024 + order[j], RANK, stride=NB), :] = total[u * RANK : (u + 1) * RANK]
        for u, j in blocks:
            mixed = [by_parity(inner, gu * 1024 + order[j]) for gu in range(2)]
            grad = nn(crossed_pair(*mixed), jnp.concatenate([sent[0][u], sent[1][u]], axis=0))
            for gu in range(2):
                for h in range(2):
                    base = h * 128 + gu * 64 + i * GROUP + u
                    for al in range(2):
                        g_out[pl.ds(base + al * HALF, 8, stride=RIGHT), :] = grad[
                            gu * RANK + al * 8 : gu * RANK + (al + 1) * 8, h * 128 : (h + 1) * 128
                        ]
        return 0

    lax.fori_loop(0, 4, step, 0)
    for r in range(CHUNKS):
        grads_out[r] = g_out[rows(chunk_of(me, r), RIGHT), :].astype(bf16)


def left_body(where, back, x, x_got, keep, send, turned):
    me, side = where[0], where[1]
    toks = back.shape[1]
    ats = [tokens_at(v, side, toks) for v in (x, x_got)]
    for b, (ref, out) in enumerate([(x, keep), (x_got, send)]):

        def step(i, _, b=b, ref=ref):
            parts = ([], [])
            for q in range(2):
                both = []
                for u in range(4 * q, 4 * q + 4):
                    j = ((side ^ b) * 4 + i) * GROUP + u
                    both += [back[rows(j), :], back[rows(j + NB), :]]
                both = jnp.concatenate(both, axis=0).astype(bf16)
                at = i * 4 + 2 * q
                x4 = jnp.concatenate([ref[ats[b], lanes(at, 256)], ref[ats[b], lanes(at + 1, 256)]], axis=0)
                grads = nn(crossed_pair(both[:64], both[64:]), x4)
                for e in range(4):
                    for gu in range(2):
                        top = (e * 2 + gu) * RANK
                        parts[gu].append(grads[top : top + RANK, (e % 2) * 128 : (e % 2 + 1) * 128])
            for gu in range(2):
                turned[rows(gu * 4 + i, 128), :] = jnp.concatenate(parts[gu], axis=0).T.astype(bf16)
            return 0

        lax.fori_loop(0, 4, step, 0)
        for r in range(CHUNKS):
            d = chunk_of(me, r)
            for gg in range(8):
                at = pl.multiple_of(gg * 128 + d * 16, 16)
                out[r, pl.ds(gg * 16, 16), :] = turned[pl.ds(at, 16), :]


VMEM = pl.BlockSpec(memory_space=pltpu.VMEM)
SMEM = pl.BlockSpec(memory_space=pltpu.SMEM)


ANY = pl.BlockSpec(memory_space=pl.ANY)
HBM = pl.BlockSpec(memory_space=pltpu.HBM)
VMEM_MIDDLE = 20 * 2**20
VMEM_RIGHT = 10 * 2**20


def prepare_call(factors):
    return pl.pallas_call(
        prepare_body,
        out_shape=jax.ShapeDtypeStruct((FIRST + REST, 128), bf16),
        in_specs=[HBM] * 6,
        out_specs=VMEM,
        scratch_shapes=[pltpu.VMEM(v.shape, bf16) for v in factors] + [pltpu.SemaphoreType.DMA((6,))],
        compiler_params=pltpu.CompilerParams(vmem_limit_bytes=60 * 2**20),
    )(*factors)


def finish_call(first, rights, downs):
    cut, count = len(first), len(first) + len(rights) + len(downs)
    turn = cut + len(rights)
    shapes = [256, 448, 256, 448, 448, 256]
    return pl.pallas_call(
        lambda *refs: finish_body(refs[:cut], refs[cut:turn], refs[turn:count], *refs[count:]),
        out_shape=tuple(jax.ShapeDtypeStruct((HALF, c), f32) for c in shapes),
        in_specs=[VMEM] * count,
        out_specs=(VMEM,) * 6,
        compiler_params=pltpu.CompilerParams(vmem_limit_bytes=16 * 2**20),
    )(*first, *rights, *downs)


def inner_call(where, along, across, x, toks):
    front = pl.BlockSpec((4, FIRST, 128), lambda i: (0, 0, 0))
    return pl.pallas_call(
        inner_body,
        grid=(1,),
        out_shape=jax.ShapeDtypeStruct((2, NB * RANK // 2, toks), f32),
        in_specs=[SMEM, front, front, VMEM],
        out_specs=VMEM,
        scratch_shapes=[pltpu.VMEM((8, BIN, 128), bf16)],
        compiler_params=pltpu.CompilerParams(vmem_limit_bytes=10 * 2**20),
        cost_estimate=pl.CostEstimate(flops=10**9, bytes_accessed=10**7, transcendentals=0),
    )(where, along, across, x)


def middle_call(scale, where, order, pieces, inner, y, y_got):
    toks = y_got.shape[0] // 2
    down = jax.ShapeDtypeStruct((CHUNKS, DOWN, 128), bf16)
    kept = jax.ShapeDtypeStruct((HALF, toks, WIDE), f32)
    return pl.pallas_call(
        functools.partial(middle_body, scale),
        out_shape=(
            down,
            down,
            jax.ShapeDtypeStruct((2 * NB * RANK, toks), f32),
            jax.ShapeDtypeStruct((NB * RANK, toks), f32),
            jax.ShapeDtypeStruct((2, GROUPS, WIDE, 128), bf16),
            jax.ShapeDtypeStruct((GROUPS, 128, WIDE), bf16),
            kept,
            kept,
            kept,
            kept,
        ),
        in_specs=[SMEM, SMEM] + [VMEM] * 8,
        out_specs=(VMEM,) * 10,
        scratch_shapes=[
            pltpu.VMEM((RANK * 128, 128), f32),
            pltpu.VMEM((RANK * 128, 128), f32),
            pltpu.VMEM((RANK * NB, 128), f32),
            pltpu.VMEM((2, GROUPS, 128, WIDE), bf16),
            pltpu.VMEM((GROUPS, 128, BIN), bf16),
            pltpu.VMEM((GROUPS, BIN, 128), bf16),
            pltpu.VMEM((GROUPS, WIDE, 128), bf16),
            pltpu.VMEM((2, CHUNKS * DOWN, 128), f32),
            pltpu.VMEM((NB * RANK, toks), f32),
            pltpu.VMEM((NB, toks, WIDE), bf16),
        ],
        compiler_params=pltpu.CompilerParams(vmem_limit_bytes=VMEM_MIDDLE),
        cost_estimate=pl.CostEstimate(flops=5 * 10**9, bytes_accessed=4 * 10**7, transcendentals=0),
    )(where, order, *pieces, *inner, y, y_got)


def right_call(b, where, order, *arrays):
    toks = arrays[0].shape[1]
    return pl.pallas_call(
        functools.partial(right_body, b),
        out_shape=(
            jax.ShapeDtypeStruct((CHUNKS, RIGHT, 128), bf16),
            jax.ShapeDtypeStruct((2 * NB * RANK, toks), f32),
        ),
        in_specs=[SMEM, SMEM] + [VMEM] * len(arrays),
        out_specs=(VMEM, VMEM),
        scratch_shapes=[pltpu.VMEM((CHUNKS * RIGHT, 128), f32)],
        compiler_params=pltpu.CompilerParams(vmem_limit_bytes=VMEM_RIGHT),
        cost_estimate=pl.CostEstimate(flops=5 * 10**9, bytes_accessed=2 * 10**7, transcendentals=0),
    )(where, order, *arrays)


def left_call(where, back, x, x_got):
    grads = jax.ShapeDtypeStruct((CHUNKS, FIRST, 128), bf16)
    return pl.pallas_call(
        left_body,
        out_shape=(grads, grads),
        in_specs=[SMEM] + [VMEM] * 3,
        out_specs=(VMEM, VMEM),
        scratch_shapes=[
            pltpu.VMEM((8 * 128, 128), bf16),
        ],
        compiler_params=pltpu.CompilerParams(vmem_limit_bytes=16 * 2**20),
        cost_estimate=pl.CostEstimate(flops=10**9, bytes_accessed=10**7, transcendentals=0),
    )(where, back, x, x_got)


def swap(v, axis, bit, size):
    return lax.ppermute(v, axis, [(i, i ^ bit) for i in range(size)])


def sibling(v):
    return swap(v, "blk", 1, 2)


def gathered(mine, n):
    z1, z2, z3 = [swap(mine, "dp", 2 * s, n) for s in range(1, 4)]
    x0, x1, x2, x3 = [swap(v, "dp", 1, n) for v in (mine, z1, z2, z3)]
    pair = (x0, x1)
    along = jnp.stack([mine, z2, z1, z3])
    across = jnp.stack([pair[0], x2, pair[1], x3])
    return (z1, z3), along, across, sibling(along), sibling(across)


def add(a, b):
    return (a.astype(f32) + b.astype(f32)).astype(bf16)


def tie(value, *others):
    return lax.optimization_barrier((value,) + others)[0]


def over_x(keep, got, n):
    away = add(keep[4:], got[4:])
    return away, swap(away, "dp", 1, n)


def line_of(keep, got, crossed):
    return (keep[:4].astype(f32) + got[:4].astype(f32) + crossed.astype(f32)).astype(bf16)


def over_z(line, n):
    return add(line[:2], swap(line[2:], "dp", 2, n))


def on_device(activations, teacher_out, block_order, *factors):
    n = lax.axis_size("dp")
    me = lax.axis_index("dp")
    side = lax.axis_index("blk")
    toks = activations.shape[0] // 2
    scale = float(activations.shape[0] * n) ** (-0.5)
    direct = n == CHUNKS
    if direct:
        where = jnp.stack([me, side]).astype(jnp.int32)
        ready, *pieces = gathered(prepare_call(factors), n)
        start = side * toks
    else:
        start = side * toks
        where = jnp.stack([jnp.zeros_like(side), side]).astype(jnp.int32)
        whole = [lax.all_gather(v, "dp", axis=1, tiled=True) for v in factors]
        cut = [jnp.moveaxis(v.reshape(HALF, CHUNKS, -1), 1, 0) for v in whole]
        packed = jnp.concatenate(jax.vmap(pack)(*cut), axis=1)
        packed = packed.reshape((4, 2) + packed.shape[1:])[jnp.array(STEPS)]
        pieces = (packed[:, 0], packed[:, 1], sibling(packed[:, 0]), sibling(packed[:, 1]))
    x, y = [lax.dynamic_slice_in_dim(v, start, toks, 0) for v in (activations, teacher_out)]
    x_got, y_got = sibling(activations), sibling(teacher_out)
    inner = (
        inner_call(where, pieces[0], pieces[1], x, toks),
        inner_call(where, pieces[2], pieces[3], x_got, toks),
    )
    keep, send, *state = middle_call(scale, where, block_order, pieces, inner, y, y_got)
    shared, (act_own, act_oth, slope_own, slope_oth) = state[:4], state[4:]
    got = sibling(send)
    right_send, back = right_call(1, where, block_order, *shared, act_oth, slope_oth)
    right_got = sibling(right_send)
    if direct:
        _, crossed = over_x(keep, got, n)
        line = line_of(keep, got, crossed)
        back = tie(back, line)
    right_keep, back = right_call(0, where, block_order, *shared, act_own, slope_own, back)
    if direct:
        half = over_z(line, n)
        right_away, right_crossed = over_x(right_keep, right_got, n)
        back = tie(back, half, right_away)
    left_keep, left_send = left_call(where, back, x, x_got)
    left_got = sibling(left_send)
    if direct:
        down = [half[0], swap(half[1], "dp", 4, n)]
        left_got = tie(left_got, down[1])
        right_half = over_z(line_of(right_keep, right_got, right_crossed), n)
        left_away = tie(add(left_keep[4:], left_got[4:]), right_crossed)
        left_crossed = swap(left_away, "dp", 1, n)
        left_half = over_z(line_of(left_keep, left_got, left_crossed), n)
        right = [right_half[0], swap(right_half[1], "dp", 4, n)]
        left = [left_half[0], swap(left_half[1], "dp", 4, n)]
        return finish_call(left, right, down)
    rest = (jnp.concatenate([right_keep, keep], axis=1), jnp.concatenate([right_got, got], axis=1))
    sums = []
    rest = [jnp.concatenate(v, axis=1) for v in ((right_keep, keep), (right_send, send))]
    for own, away in ((left_keep, left_got), rest):
        total = own.astype(f32) + away.astype(f32)
        ranks = jnp.array(STEPS)
        sums.append(jnp.stack([total[:4][ranks], total[4:][ranks]], axis=1).reshape(total.shape))
    parts = jax.vmap(unpack)(*sums)
    parts = [jnp.moveaxis(v, 0, 1).reshape(HALF, -1) for v in parts]
    return tuple(lax.psum_scatter(v, "dp", scatter_dimension=1, tiled=True) for v in parts)


def solution(mesh):
    tokens = P(("group", "dp"), "blk")
    factor = P("blk", "dp")
    grad = P(("group", "blk"), "dp")
    return jax.shard_map(
        on_device,
        mesh=mesh,
        in_specs=(tokens, tokens, P()) + (factor,) * 6,
        out_specs=(grad,) * 6,
        check_vma=False,
    )
```

```python
import functools

import jax
import jax.numpy as jnp
from jax import lax
from jax.experimental import pallas as pl
from jax.experimental.pallas import tpu as pltpu
from jax.sharding import PartitionSpec as P

NB = 64
HALF = 32
RANK = 16
BIN = 128
BHID = 224
WIDE = 256
CHUNKS = 8
GROUP = 8
GROUPS = NB // GROUP
f32 = jnp.float32
bf16 = jnp.bfloat16

STEPS = (0, 2, 1, 3)
FIRST = 128
REST = 448
RD_AT = 256
LD_AT = 320
RIGHT = 256
DOWN = 192


def pack(lg, rg, lu, ru, ld, rd):
    left = jnp.stack([lg, lu]).reshape(2, 4, 8, 16, 16)
    left = jnp.transpose(left, (0, 1, 3, 2, 4)).reshape(FIRST, 128)
    right = jnp.stack([rg, ru]).reshape(2, HALF, 2, 8, 28)
    right = jnp.pad(right, ((0, 0),) * 4 + ((0, 4),)).reshape(2, HALF, 2, 2, 128)
    right = jnp.transpose(right, (3, 0, 2, 1, 4)).reshape(256, 128)
    rdown = jnp.transpose(rd.reshape(HALF, 2, 128), (1, 0, 2)).reshape(64, 128)
    ldown = jnp.transpose(ld.reshape(4, 8, 28, 16), (0, 2, 1, 3)).reshape(4, 28, 128)
    ldown = jnp.pad(ldown, ((0, 0), (0, 4), (0, 0))).reshape(128, 128)
    return left, jnp.concatenate([right, rdown, ldown], axis=0)


def unpack(first, rest):
    left = jnp.transpose(first.reshape(2, 4, 16, 8, 16), (0, 1, 3, 2, 4)).reshape(2, HALF, 256)
    right = jnp.transpose(rest[:RD_AT].reshape(2, 2, 2, HALF, 128), (1, 3, 2, 0, 4))
    right = right.reshape(2, HALF, 2, 8, 32)[..., :28].reshape(2, HALF, 448)
    rdown = jnp.transpose(rest[RD_AT:LD_AT].reshape(2, HALF, 128), (1, 0, 2)).reshape(HALF, 256)
    ldown = rest[LD_AT:].reshape(4, 32, 8, 16)[:, :28]
    ldown = jnp.transpose(ldown, (0, 2, 1, 3)).reshape(HALF, 448)
    return left[0], right[0], left[1], right[1], ldown, rdown


def turn_blocks(v):
    whole = v.reshape(-1, 8, 128)
    row = lax.broadcasted_iota(jnp.int32, (1, 8, 128), 1)
    lane = lax.broadcasted_iota(jnp.int32, (1, 8, 128), 2) // RANK
    out = whole
    for s in range(1, 8):
        moved = pltpu.roll(pltpu.roll(whole, s, 1), 128 - RANK * s, 2)
        out = jnp.where((row - lane - s) % 8 == 0, moved, out)
    return out


def spaced(v):
    gap = jnp.zeros((v.shape[0], 4), f32)
    parts = []
    for q in range(8):
        parts += [v[:, 28 * q : 28 * q + 28], gap]
    return jnp.concatenate(parts, axis=1)


def prepare_body(*refs):
    shards, packed, (lg, rg, lu, ru, ld, rd), sems = refs[:6], refs[6], refs[7:13], refs[13]
    loads = [
        pltpu.make_async_copy(shard, ref, sems.at[i]) for i, (shard, ref) in enumerate(zip(shards, refs[7:13]))
    ]
    for copy in loads:
        copy.start()
    for copy in loads:
        copy.wait()
    for gu, ref in enumerate([lg, lu]):
        v = ref[...].astype(f32)
        lo, hi = turn_blocks(v[:, :128]), turn_blocks(v[:, 128:])
        for g in range(4):
            both = jnp.concatenate([lo[g], hi[g]], axis=0)
            packed[pl.ds((gu * 4 + g) * 16, 16), :] = both.astype(bf16)
    for gu, ref in enumerate([rg, ru]):
        v = ref[...].astype(f32)
        for al in range(2):
            part = spaced(v[:, al * BHID : (al + 1) * BHID]).astype(bf16)
            for h in range(2):
                at = FIRST + h * 128 + gu * 64 + al * HALF
                packed[pl.ds(at, HALF), :] = part[:, h * 128 : (h + 1) * 128]
    for al in range(2):
        packed[pl.ds(FIRST + RD_AT + al * HALF, HALF), :] = rd[:, pl.ds(al * 128, 128)]
    v = ld[...].astype(f32)
    v = jnp.concatenate([v, jnp.zeros((HALF, 64), f32)], axis=1)
    quarters = [turn_blocks(v[:, q * 128 : (q + 1) * 128]) for q in range(4)]
    for g in range(4):
        part = jnp.concatenate([q[g] for q in quarters], axis=0).astype(bf16)
        packed[pl.ds(FIRST + LD_AT + g * 32, 32), :] = part


def finish_body(first, rights, downs, lg, rg, lu, ru, ld, rd):
    def total(pieces, start, height):
        return sum(p[pl.ds(start, height), :].astype(f32) for p in pieces)

    left = total(first, 0, FIRST)
    for gu, ref in enumerate([lg, lu]):
        v = left[gu * 64 : (gu + 1) * 64].reshape(4, 2, 8, 128)
        for h in range(2):
            ref[:, pl.ds(h * 128, 128)] = turn_blocks(v[:, h]).reshape(HALF, 128)
    right = total(rights, 0, RIGHT)
    for gu, ref in enumerate([rg, ru]):
        parts = []
        for al in range(2):
            for q in range(8):
                at = (q // 4) * 128 + gu * 64 + al * HALF
                parts.append(right[at : at + HALF, 32 * (q % 4) : 32 * (q % 4) + 28])
        ref[...] = jnp.concatenate(parts, axis=1)
    down = total(downs, 0, 64)
    for al in range(2):
        rd[:, pl.ds(al * 128, 128)] = down[al * HALF : (al + 1) * HALF]
    v = total(downs, 64, 128).reshape(4, 4, 8, 128)
    parts = [turn_blocks(v[:, q]).reshape(HALF, 128) for q in range(4)]
    ld[...] = jnp.concatenate(parts, axis=1)[:, :448]


def nn(a, b):
    return jnp.dot(a, b, preferred_element_type=f32)


def rounded(v):
    return v.astype(bf16).astype(f32)


def rows(j, height=RANK):
    return pl.ds(pl.multiple_of(j * height, height), height)


def lanes(j, width=BIN):
    return pl.ds(pl.multiple_of(j * width, width), width)


def spread(v, masks):
    return jnp.concatenate([v * mask for mask in masks], axis=0)


def chosen(out, toks):
    slot = lax.broadcasted_iota(jnp.int32, (toks, 128), 1) // RANK
    total = out[:toks]
    for u in range(1, GROUP):
        total = jnp.where(slot == u, out[u * toks : (u + 1) * toks], total)
    return total


def crossed_pair(a, b):
    return jnp.concatenate(
        [jnp.concatenate([a, jnp.zeros_like(b)], axis=1), jnp.concatenate([jnp.zeros_like(a), b], axis=1)], axis=0
    )


def unit_masks():
    slot = lax.broadcasted_iota(jnp.int32, (1, 128), 1) // RANK
    return [jnp.where(slot == u, 1.0, 0.0).astype(bf16) for u in range(GROUP)]


def tokens_at(ref, side, toks):
    return pl.ds(0, toks) if ref.shape[0] == toks else pl.ds(pl.multiple_of(side * toks, toks), toks)


def chunk_of(me, r):
    return me ^ (2 * STEPS[r % 4]) ^ (r // 4)


def inner_body(where, along, across, x, inner, t_l):
    me = where[0]
    toks = inner.shape[2]
    at = tokens_at(x, where[1], toks)
    masks = [jnp.concatenate([mask, mask], axis=1) for mask in unit_masks()]
    for r in range(CHUNKS):
        piece = (along, across)[r // 4]
        for gg in range(8):
            t_l[gg, rows(chunk_of(me, r)), :] = piece[r % 4, pl.ds(gg * 16, 16), :]

    def step(i, _):
        both = jnp.concatenate([t_l[i], t_l[4 + i]], axis=1)
        total = jnp.zeros((toks, 256), f32)
        for p in range(GROUP // 2):
            w = jnp.concatenate([both * masks[2 * p + h] for h in range(2)], axis=0)
            total += nn(x[at, lanes(i * GROUP // 2 + p, 256)], w)
        for gu in range(2):
            inner[gu, rows(i, 128), :] = rounded(total[:, gu * 128 : (gu + 1) * 128].T)
        return 0

    lax.fori_loop(0, 4, step, 0)


def by_parity(ref, m):
    return jnp.concatenate(
        [ref[pl.ds(m, 8, stride=2 * NB), :], ref[pl.ds(m + NB, 8, stride=2 * NB), :]], axis=0
    ).astype(bf16)


def middle_body(
    scale, where, order, own_a, own_b, oth_a, oth_b, inner_own, inner_oth, y, y_got, keep, send,
    inner, ret, t_r, n_ld, act_own, act_oth, slope_own, slope_oth,
    r_lo, r_hi, s_rd, n_r, n_rd, t_rd, t_ld, g_out, down, hid_s,
):
    me, side = where[0], where[1]
    toks = inner.shape[1]
    ats = [tokens_at(v, side, toks) for v in (y, y_got)]
    masks = unit_masks()
    s_r = (r_lo, r_hi)
    for gu in range(2):
        for b, part in enumerate([inner_own, inner_oth]):
            inner[rows(gu * 2 + (side ^ b), 512), :] = part[gu]

    for b, pieces in enumerate([(own_a, own_b), (oth_a, oth_b)]):
        blk = side ^ b
        for r in range(CHUNKS):
            d = chunk_of(me, r)
            ref, at = pieces[r // 4], r % 4
            for gu in range(2):
                for al in range(2):
                    row = pl.multiple_of((2 * d + al) * 128 + gu * NB + blk * HALF, HALF)
                    for half in range(2):
                        src = FIRST + half * 128 + gu * 64 + al * HALF
                        s_r[half][pl.ds(row, HALF), :] = ref[at, pl.ds(src, HALF), :].astype(f32)
            for al in range(2):
                row = pl.multiple_of((2 * d + al) * NB + blk * HALF, HALF)
                s_rd[pl.ds(row, HALF), :] = ref[at, pl.ds(FIRST + RD_AT + al * HALF, HALF), :].astype(f32)
            for g in range(4):
                t_ld[blk * 4 + g, rows(d, 32), :] = ref[at, pl.ds(FIRST + LD_AT + g * 32, 32), :]

    def stacked(ref, start, stride, g):
        return jnp.concatenate(
            [ref[pl.ds(start + g * GROUP + u, RANK, stride=stride), :] for u in range(GROUP)], axis=0
        )

    def turn(g, _):
        for gu in range(2):
            for h in range(2):
                flat = stacked(s_r[h], gu * NB, 128, g)
                n_r[gu, g, :, pl.ds(h * 128, 128)] = flat.astype(bf16)
                t_r[gu, g, pl.ds(h * 128, 128), :] = flat.astype(bf16).T
        for h in range(2):
            n_ld[g, :, pl.ds(h * 128, 128)] = t_ld[g, pl.ds(h * 128, 128), :].T
        flat = stacked(s_rd, 0, NB, g)
        n_rd[g] = flat.astype(bf16)
        t_rd[g] = flat.astype(bf16).T
        return 0

    lax.fori_loop(0, GROUPS, turn, 0)

    def blocks(g):
        return [(u, g * GROUP + u) for u in range(GROUP)]

    def second(i, _, b):
        g = (side ^ b) * 4 + i
        act_s, slope_s = ((act_own, slope_own), (act_oth, slope_oth))[b]
        turned = []
        for gu in range(2):
            mixed = [inner[pl.ds(gu * 1024 + order[k], RANK, stride=NB), :] for u, k in blocks(g)]
            turned.append(jnp.concatenate(mixed, axis=0).T.astype(bf16))
        span = pl.ds(pl.multiple_of(i * GROUP, GROUP), GROUP)
        act_s[span] = nn(spread(turned[0], masks), n_r[0, g]).reshape(GROUP, toks, WIDE)
        slope_s[span] = nn(spread(turned[1], masks), n_r[1, g]).reshape(GROUP, toks, WIDE)
        for u, k in blocks(g):
            local = i * GROUP + u
            gate, upper = act_s[local], slope_s[local]
            sig = 0.5 * jnp.tanh(0.5 * gate) + 0.5
            act = gate * sig
            act_s[local] = act
            slope_s[local] = upper * (sig + act * (1.0 - sig))
            hid_s[k] = (act * upper).astype(bf16)
        hidden = hid_s[pl.ds(pl.multiple_of(g * GROUP, GROUP), GROUP)].reshape(GROUP * toks, WIDE)
        total = chosen(nn(hidden, t_ld[g]), toks)
        down[rows(g, 128), :] = rounded(total.T)
        return 0

    for b in range(2):
        lax.fori_loop(0, 4, functools.partial(second, b=b), 0)

    def put(b, base, value):
        for al in range(2):
            g_out[b, pl.ds(base + al * HALF, 8, stride=DOWN), :] = value[al * 8 : (al + 1) * 8]

    for b in range(2):

        def third(i, _, b=b):
            g = (side ^ b) * 4 + i
            dms = [down[pl.ds(order[k], RANK, stride=NB), :] for u, k in blocks(g)]
            turned = jnp.concatenate(dms, axis=0).T.astype(bf16)
            student = nn(spread(turned, masks), n_rd[g])
            deltas = []
            for u, k in blocks(g):
                target = (y, y_got)[b][ats[b], lanes(i * GROUP + u)].astype(f32)
                part = student[u * toks : (u + 1) * toks]
                deltas.append(((part - target) * scale).astype(bf16))
            total = chosen(nn(jnp.concatenate(deltas, axis=0), t_rd[g]), toks)
            parity = [by_parity(down, order[k]) for u, k in blocks(g)]
            for q in range(2):
                d = deltas[4 * q : 4 * q + 4]
                m = parity[4 * q : 4 * q + 4]
                grads = nn(
                    crossed_pair(jnp.concatenate(m[:2], axis=0), jnp.concatenate(m[2:], axis=0)),
                    jnp.concatenate([jnp.concatenate(d[:2], axis=1), jnp.concatenate(d[2:], axis=1)], axis=0),
                )
                for e in range(4):
                    part = grads[e * RANK : (e + 1) * RANK, (e % 2) * 128 : (e % 2 + 1) * 128]
                    put(b, i * GROUP + 4 * q + e, part)
            total = rounded(total.T)
            for u, k in blocks(g):
                ret[pl.ds(order[k], RANK, stride=NB), :] = total[u * RANK : (u + 1) * RANK]
            return 0

        lax.fori_loop(0, 4, third, 0)

    def inward(i, _, b):
        g = (side ^ b) * 4 + i
        returned = ret[rows(g, 128), :].astype(bf16)
        grads = []
        for p in range(GROUP // 2):
            pair = [returned[u * RANK : (u + 1) * RANK] for u in (2 * p, 2 * p + 1)]
            both = hid_s[pl.ds(g * GROUP + 2 * p, 2)].reshape(2 * toks, WIDE)
            grads.append(nn(crossed_pair(*pair), both))
        grads = jnp.concatenate(grads, axis=0)
        for h in range(2):
            part = grads[:, h * 128 : (h + 1) * 128].T
            for q in range(4):
                at = (h * 4 + q) * DOWN + 64 + i * 32
                g_out[b, pl.ds(pl.multiple_of(at, 32), 32), :] = part[q * 32 : (q + 1) * 32]
        return 0

    for b in range(2):
        lax.fori_loop(0, 4, functools.partial(inward, b=b), 0)

    for b, out in enumerate([keep, send]):
        for r in range(CHUNKS):
            out[r] = g_out[b, rows(chunk_of(me, r), DOWN), :].astype(bf16)


def right_body(b, where, order, inner, ret, t_r, n_ld, act_s, slope_s, *refs):
    if b == 0:
        before, grads_out, back, g_out = refs
        back[...] = before[...]
    else:
        grads_out, back, g_out = refs
    me, side = where[0], where[1]
    toks = inner.shape[1]
    masks = unit_masks()

    def step(i, _):
        g = (side ^ b) * 4 + i
        blocks = [(u, g * GROUP + u) for u in range(GROUP)]
        turned = ret[rows(g, 128), :].T.astype(bf16)
        dhidden = nn(spread(turned, masks), n_ld[g])
        sent = ([], [])
        for u, j in blocks:
            local, part = i * GROUP + u, dhidden[u * toks : (u + 1) * toks]
            sent[0].append((part * slope_s[local]).astype(bf16))
            sent[1].append((part * act_s[local]).astype(bf16))
        for gu in range(2):
            total = rounded(chosen(nn(jnp.concatenate(sent[gu], axis=0), t_r[gu, g]), toks).T)
            for u, j in blocks:
                back[pl.ds(gu * 1024 + order[j], RANK, stride=NB), :] = total[u * RANK : (u + 1) * RANK]
        for u, j in blocks:
            mixed = [by_parity(inner, gu * 1024 + order[j]) for gu in range(2)]
            grad = nn(crossed_pair(*mixed), jnp.concatenate([sent[0][u], sent[1][u]], axis=0))
            for gu in range(2):
                for h in range(2):
                    base = h * 128 + gu * 64 + i * GROUP + u
                    for al in range(2):
                        g_out[pl.ds(base + al * HALF, 8, stride=RIGHT), :] = grad[
                            gu * RANK + al * 8 : gu * RANK + (al + 1) * 8, h * 128 : (h + 1) * 128
                        ]
        return 0

    lax.fori_loop(0, 4, step, 0)
    for r in range(CHUNKS):
        grads_out[r] = g_out[rows(chunk_of(me, r), RIGHT), :].astype(bf16)


def left_body(where, back, x, x_got, keep, send, turned):
    me, side = where[0], where[1]
    toks = back.shape[1]
    ats = [tokens_at(v, side, toks) for v in (x, x_got)]
    for b, (ref, out) in enumerate([(x, keep), (x_got, send)]):

        def step(i, _, b=b, ref=ref):
            parts = ([], [])
            for q in range(2):
                both = []
                for u in range(4 * q, 4 * q + 4):
                    j = ((side ^ b) * 4 + i) * GROUP + u
                    both += [back[rows(j), :], back[rows(j + NB), :]]
                both = jnp.concatenate(both, axis=0).astype(bf16)
                at = i * 4 + 2 * q
                x4 = jnp.concatenate([ref[ats[b], lanes(at, 256)], ref[ats[b], lanes(at + 1, 256)]], axis=0)
                grads = nn(crossed_pair(both[:64], both[64:]), x4)
                for e in range(4):
                    for gu in range(2):
                        top = (e * 2 + gu) * RANK
                        parts[gu].append(grads[top : top + RANK, (e % 2) * 128 : (e % 2 + 1) * 128])
            for gu in range(2):
                turned[rows(gu * 4 + i, 128), :] = jnp.concatenate(parts[gu], axis=0).T.astype(bf16)
            return 0

        lax.fori_loop(0, 4, step, 0)
        for r in range(CHUNKS):
            d = chunk_of(me, r)
            for gg in range(8):
                at = pl.multiple_of(gg * 128 + d * 16, 16)
                out[r, pl.ds(gg * 16, 16), :] = turned[pl.ds(at, 16), :]


VMEM = pl.BlockSpec(memory_space=pltpu.VMEM)
SMEM = pl.BlockSpec(memory_space=pltpu.SMEM)


ANY = pl.BlockSpec(memory_space=pl.ANY)
HBM = pl.BlockSpec(memory_space=pltpu.HBM)
VMEM_MIDDLE = 20 * 2**20
VMEM_RIGHT = 10 * 2**20


def prepare_call(factors):
    return pl.pallas_call(
        prepare_body,
        out_shape=jax.ShapeDtypeStruct((FIRST + REST, 128), bf16),
        in_specs=[HBM] * 6,
        out_specs=VMEM,
        scratch_shapes=[pltpu.VMEM(v.shape, bf16) for v in factors] + [pltpu.SemaphoreType.DMA((6,))],
        compiler_params=pltpu.CompilerParams(vmem_limit_bytes=60 * 2**20),
    )(*factors)


def finish_call(first, rights, downs):
    cut, count = len(first), len(first) + len(rights) + len(downs)
    turn = cut + len(rights)
    shapes = [256, 448, 256, 448, 448, 256]
    return pl.pallas_call(
        lambda *refs: finish_body(refs[:cut], refs[cut:turn], refs[turn:count], *refs[count:]),
        out_shape=tuple(jax.ShapeDtypeStruct((HALF, c), f32) for c in shapes),
        in_specs=[VMEM] * count,
        out_specs=(VMEM,) * 6,
        compiler_params=pltpu.CompilerParams(vmem_limit_bytes=16 * 2**20),
    )(*first, *rights, *downs)


def inner_call(where, along, across, x, toks):
    front = pl.BlockSpec((4, FIRST, 128), lambda i: (0, 0, 0))
    return pl.pallas_call(
        inner_body,
        grid=(1,),
        out_shape=jax.ShapeDtypeStruct((2, NB * RANK // 2, toks), f32),
        in_specs=[SMEM, front, front, VMEM],
        out_specs=VMEM,
        scratch_shapes=[pltpu.VMEM((8, BIN, 128), bf16)],
        compiler_params=pltpu.CompilerParams(vmem_limit_bytes=10 * 2**20),
        cost_estimate=pl.CostEstimate(flops=10**9, bytes_accessed=10**7, transcendentals=0),
    )(where, along, across, x)


def middle_call(scale, where, order, pieces, inner, y, y_got):
    toks = y_got.shape[0] // 2
    down = jax.ShapeDtypeStruct((CHUNKS, DOWN, 128), bf16)
    kept = jax.ShapeDtypeStruct((HALF, toks, WIDE), f32)
    return pl.pallas_call(
        functools.partial(middle_body, scale),
        out_shape=(
            down,
            down,
            jax.ShapeDtypeStruct((2 * NB * RANK, toks), f32),
            jax.ShapeDtypeStruct((NB * RANK, toks), f32),
            jax.ShapeDtypeStruct((2, GROUPS, WIDE, 128), bf16),
            jax.ShapeDtypeStruct((GROUPS, 128, WIDE), bf16),
            kept,
            kept,
            kept,
            kept,
        ),
        in_specs=[SMEM, SMEM] + [VMEM] * 8,
        out_specs=(VMEM,) * 10,
        scratch_shapes=[
            pltpu.VMEM((RANK * 128, 128), f32),
            pltpu.VMEM((RANK * 128, 128), f32),
            pltpu.VMEM((RANK * NB, 128), f32),
            pltpu.VMEM((2, GROUPS, 128, WIDE), bf16),
            pltpu.VMEM((GROUPS, 128, BIN), bf16),
            pltpu.VMEM((GROUPS, BIN, 128), bf16),
            pltpu.VMEM((GROUPS, WIDE, 128), bf16),
            pltpu.VMEM((2, CHUNKS * DOWN, 128), f32),
            pltpu.VMEM((NB * RANK, toks), f32),
            pltpu.VMEM((NB, toks, WIDE), bf16),
        ],
        compiler_params=pltpu.CompilerParams(vmem_limit_bytes=VMEM_MIDDLE),
        cost_estimate=pl.CostEstimate(flops=5 * 10**9, bytes_accessed=4 * 10**7, transcendentals=0),
    )(where, order, *pieces, *inner, y, y_got)


def right_call(b, where, order, *arrays):
    toks = arrays[0].shape[1]
    return pl.pallas_call(
        functools.partial(right_body, b),
        out_shape=(
            jax.ShapeDtypeStruct((CHUNKS, RIGHT, 128), bf16),
            jax.ShapeDtypeStruct((2 * NB * RANK, toks), f32),
        ),
        in_specs=[SMEM, SMEM] + [VMEM] * len(arrays),
        out_specs=(VMEM, VMEM),
        scratch_shapes=[pltpu.VMEM((CHUNKS * RIGHT, 128), f32)],
        compiler_params=pltpu.CompilerParams(vmem_limit_bytes=VMEM_RIGHT),
        cost_estimate=pl.CostEstimate(flops=5 * 10**9, bytes_accessed=2 * 10**7, transcendentals=0),
    )(where, order, *arrays)


def left_call(where, back, x, x_got):
    grads = jax.ShapeDtypeStruct((CHUNKS, FIRST, 128), bf16)
    return pl.pallas_call(
        left_body,
        out_shape=(grads, grads),
        in_specs=[SMEM] + [VMEM] * 3,
        out_specs=(VMEM, VMEM),
        scratch_shapes=[
            pltpu.VMEM((8 * 128, 128), bf16),
        ],
        compiler_params=pltpu.CompilerParams(vmem_limit_bytes=16 * 2**20),
        cost_estimate=pl.CostEstimate(flops=10**9, bytes_accessed=10**7, transcendentals=0),
    )(where, back, x, x_got)


def swap(v, axis, bit, size):
    return lax.ppermute(v, axis, [(i, i ^ bit) for i in range(size)])


def sibling(v):
    return swap(v, "blk", 1, 2)


def gathered(mine, n):
    z1, z2, z3 = [swap(mine, "dp", 2 * s, n) for s in range(1, 4)]
    x0, x1, x2, x3 = [swap(v, "dp", 1, n) for v in (mine, z1, z2, z3)]
    pair = (x0, x1)
    along = jnp.stack([mine, z2, z1, z3])
    across = jnp.stack([pair[0], x2, pair[1], x3])
    return along, across, sibling(along), sibling(across)


def add(a, b):
    return (a.astype(f32) + b.astype(f32)).astype(bf16)


def tie(value, *others):
    return lax.optimization_barrier((value,) + others)[0]


def over_x(keep, got, n):
    away = add(keep[4:], got[4:])
    return away, swap(away, "dp", 1, n)


def line_of(keep, got, crossed):
    return (keep[:4].astype(f32) + got[:4].astype(f32) + crossed.astype(f32)).astype(bf16)


def over_z(line, n):
    return add(line[:2], swap(line[2:], "dp", 2, n))


def on_device(activations, teacher_out, block_order, *factors):
    n = lax.axis_size("dp")
    me = lax.axis_index("dp")
    side = lax.axis_index("blk")
    toks = activations.shape[0] // 2
    scale = float(activations.shape[0] * n) ** (-0.5)
    direct = n == CHUNKS
    if direct:
        where = jnp.stack([me, side]).astype(jnp.int32)
        pieces = gathered(prepare_call(factors), n)
    else:
        where = jnp.stack([jnp.zeros_like(side), side]).astype(jnp.int32)
        whole = [lax.all_gather(v, "dp", axis=1, tiled=True) for v in factors]
        cut = [jnp.moveaxis(v.reshape(HALF, CHUNKS, -1), 1, 0) for v in whole]
        packed = jnp.concatenate(jax.vmap(pack)(*cut), axis=1)
        packed = packed.reshape((4, 2) + packed.shape[1:])[jnp.array(STEPS)]
        pieces = (packed[:, 0], packed[:, 1], sibling(packed[:, 0]), sibling(packed[:, 1]))
    x, y = [lax.dynamic_slice_in_dim(v, side * toks, toks, 0) for v in (activations, teacher_out)]
    x_got, y_got = sibling(activations), sibling(teacher_out)
    inner = (
        inner_call(where, pieces[0], pieces[1], x, toks),
        inner_call(where, pieces[2], pieces[3], x_got, toks),
    )
    keep, send, *state = middle_call(scale, where, block_order, pieces, inner, y, y_got)
    shared, (act_own, act_oth, slope_own, slope_oth) = state[:4], state[4:]
    got = sibling(send)
    right_send, back = right_call(1, where, block_order, *shared, act_oth, slope_oth)
    right_got = sibling(right_send)
    if direct:
        away, crossed = over_x(keep, tie(got, back), n)
        back = tie(back, away)
    right_keep, back = right_call(0, where, block_order, *shared, act_own, slope_own, back)
    if direct:
        right_away, right_crossed = over_x(right_keep, right_got, n)
        back = tie(back, right_away)
    left_keep, left_send = left_call(where, back, x, x_got)
    left_got = sibling(left_send)
    if direct:
        half = over_z(line_of(keep, got, crossed), n)
        left_away = add(left_keep[4:], left_got[4:])
        left_crossed = swap(left_away, "dp", 1, n)
        right_half = over_z(tie(line_of(right_keep, right_got, right_crossed), left_away), n)
        down = [half[0], swap(half[1], "dp", 4, n)]
        left_half = over_z(line_of(left_keep, left_got, left_crossed), n)
        right = [right_half[0], swap(tie(right_half[1], half), "dp", 4, n)]
        left = [left_half[0], swap(tie(left_half[1], right_half), "dp", 4, n)]
        return finish_call(left, right, down)
    rest = (jnp.concatenate([right_keep, keep], axis=1), jnp.concatenate([right_got, got], axis=1))
    sums = []
    rest = [jnp.concatenate(v, axis=1) for v in ((right_keep, keep), (right_send, send))]
    for own, away in ((left_keep, left_got), rest):
        total = own.astype(f32) + away.astype(f32)
        ranks = jnp.array(STEPS)
        sums.append(jnp.stack([total[:4][ranks], total[4:][ranks]], axis=1).reshape(total.shape))
    parts = jax.vmap(unpack)(*sums)
    parts = [jnp.moveaxis(v, 0, 1).reshape(HALF, -1) for v in parts]
    return tuple(lax.psum_scatter(v, "dp", scatter_dimension=1, tiled=True) for v in parts)


def solution(mesh):
    tokens = P(("group", "dp"), "blk")
    factor = P("blk", "dp")
    grad = P(("group", "blk"), "dp")
    return jax.shard_map(
        on_device,
        mesh=mesh,
        in_specs=(tokens, tokens, P()) + (factor,) * 6,
        out_specs=(grad,) * 6,
        check_vma=False,
    )
```

```python
import functools

import jax
import jax.numpy as jnp
from jax import lax
from jax.experimental import pallas as pl
from jax.experimental.pallas import tpu as pltpu
from jax.sharding import PartitionSpec as P

NB = 64
HALF = 32
RANK = 16
BIN = 128
BHID = 224
WIDE = 256
CHUNKS = 8
GROUP = 8
GROUPS = NB // GROUP
f32 = jnp.float32
bf16 = jnp.bfloat16

STEPS = (0, 2, 1, 3)
FIRST = 128
REST = 448
RD_AT = 256
LD_AT = 320
RIGHT = 256
DOWN = 192


def pack(lg, rg, lu, ru, ld, rd):
    left = jnp.stack([lg, lu]).reshape(2, 4, 8, 16, 16)
    left = jnp.transpose(left, (0, 1, 3, 2, 4)).reshape(FIRST, 128)
    right = jnp.stack([rg, ru]).reshape(2, HALF, 2, 8, 28)
    right = jnp.pad(right, ((0, 0),) * 4 + ((0, 4),)).reshape(2, HALF, 2, 2, 128)
    right = jnp.transpose(right, (3, 0, 2, 1, 4)).reshape(256, 128)
    rdown = jnp.transpose(rd.reshape(HALF, 2, 128), (1, 0, 2)).reshape(64, 128)
    ldown = jnp.transpose(ld.reshape(4, 8, 28, 16), (0, 2, 1, 3)).reshape(4, 28, 128)
    ldown = jnp.pad(ldown, ((0, 0), (0, 4), (0, 0))).reshape(128, 128)
    return left, jnp.concatenate([right, rdown, ldown], axis=0)


def unpack(first, rest):
    left = jnp.transpose(first.reshape(2, 4, 16, 8, 16), (0, 1, 3, 2, 4)).reshape(2, HALF, 256)
    right = jnp.transpose(rest[:RD_AT].reshape(2, 2, 2, HALF, 128), (1, 3, 2, 0, 4))
    right = right.reshape(2, HALF, 2, 8, 32)[..., :28].reshape(2, HALF, 448)
    rdown = jnp.transpose(rest[RD_AT:LD_AT].reshape(2, HALF, 128), (1, 0, 2)).reshape(HALF, 256)
    ldown = rest[LD_AT:].reshape(4, 32, 8, 16)[:, :28]
    ldown = jnp.transpose(ldown, (0, 2, 1, 3)).reshape(HALF, 448)
    return left[0], right[0], left[1], right[1], ldown, rdown


def turn_blocks(v):
    whole = v.reshape(-1, 8, 128)
    row = lax.broadcasted_iota(jnp.int32, (1, 8, 128), 1)
    lane = lax.broadcasted_iota(jnp.int32, (1, 8, 128), 2) // RANK
    out = whole
    for s in range(1, 8):
        moved = pltpu.roll(pltpu.roll(whole, s, 1), 128 - RANK * s, 2)
        out = jnp.where((row - lane - s) % 8 == 0, moved, out)
    return out


def spaced(v):
    gap = jnp.zeros((v.shape[0], 4), f32)
    parts = []
    for q in range(8):
        parts += [v[:, 28 * q : 28 * q + 28], gap]
    return jnp.concatenate(parts, axis=1)


def prepare_body(*refs):
    shards, packed, (lg, rg, lu, ru, ld, rd), sems = refs[:6], refs[6], refs[7:13], refs[13]
    loads = [
        pltpu.make_async_copy(shard, ref, sems.at[i]) for i, (shard, ref) in enumerate(zip(shards, refs[7:13]))
    ]
    for copy in loads:
        copy.start()
    for copy in loads:
        copy.wait()
    for gu, ref in enumerate([lg, lu]):
        v = ref[...].astype(f32)
        lo, hi = turn_blocks(v[:, :128]), turn_blocks(v[:, 128:])
        for g in range(4):
            both = jnp.concatenate([lo[g], hi[g]], axis=0)
            packed[pl.ds((gu * 4 + g) * 16, 16), :] = both.astype(bf16)
    for gu, ref in enumerate([rg, ru]):
        v = ref[...].astype(f32)
        for al in range(2):
            part = spaced(v[:, al * BHID : (al + 1) * BHID]).astype(bf16)
            for h in range(2):
                at = FIRST + h * 128 + gu * 64 + al * HALF
                packed[pl.ds(at, HALF), :] = part[:, h * 128 : (h + 1) * 128]
    for al in range(2):
        packed[pl.ds(FIRST + RD_AT + al * HALF, HALF), :] = rd[:, pl.ds(al * 128, 128)]
    v = ld[...].astype(f32)
    v = jnp.concatenate([v, jnp.zeros((HALF, 64), f32)], axis=1)
    quarters = [turn_blocks(v[:, q * 128 : (q + 1) * 128]) for q in range(4)]
    for g in range(4):
        part = jnp.concatenate([q[g] for q in quarters], axis=0).astype(bf16)
        packed[pl.ds(FIRST + LD_AT + g * 32, 32), :] = part


def finish_body(first, rights, downs, lg, rg, lu, ru, ld, rd):
    def total(pieces, start, height):
        return sum(p[pl.ds(start, height), :].astype(f32) for p in pieces)

    left = total(first, 0, FIRST)
    for gu, ref in enumerate([lg, lu]):
        v = left[gu * 64 : (gu + 1) * 64].reshape(4, 2, 8, 128)
        for h in range(2):
            ref[:, pl.ds(h * 128, 128)] = turn_blocks(v[:, h]).reshape(HALF, 128)
    right = total(rights, 0, RIGHT)
    for gu, ref in enumerate([rg, ru]):
        parts = []
        for al in range(2):
            for q in range(8):
                at = (q // 4) * 128 + gu * 64 + al * HALF
                parts.append(right[at : at + HALF, 32 * (q % 4) : 32 * (q % 4) + 28])
        ref[...] = jnp.concatenate(parts, axis=1)
    down = total(downs, 0, 64)
    for al in range(2):
        rd[:, pl.ds(al * 128, 128)] = down[al * HALF : (al + 1) * HALF]
    v = total(downs, 64, 128).reshape(4, 4, 8, 128)
    parts = [turn_blocks(v[:, q]).reshape(HALF, 128) for q in range(4)]
    ld[...] = jnp.concatenate(parts, axis=1)[:, :448]


def nn(a, b):
    return jnp.dot(a, b, preferred_element_type=f32)


def rounded(v):
    return v.astype(bf16).astype(f32)


def rows(j, height=RANK):
    return pl.ds(pl.multiple_of(j * height, height), height)


def lanes(j, width=BIN):
    return pl.ds(pl.multiple_of(j * width, width), width)


def spread(v, masks):
    return jnp.concatenate([v * mask for mask in masks], axis=0)


def chosen(out, toks):
    slot = lax.broadcasted_iota(jnp.int32, (toks, 128), 1) // RANK
    total = out[:toks]
    for u in range(1, GROUP):
        total = jnp.where(slot == u, out[u * toks : (u + 1) * toks], total)
    return total


def crossed_pair(a, b):
    return jnp.concatenate(
        [jnp.concatenate([a, jnp.zeros_like(b)], axis=1), jnp.concatenate([jnp.zeros_like(a), b], axis=1)], axis=0
    )


def unit_masks():
    slot = lax.broadcasted_iota(jnp.int32, (1, 128), 1) // RANK
    return [jnp.where(slot == u, 1.0, 0.0).astype(bf16) for u in range(GROUP)]


def tokens_at(ref, side, toks):
    return pl.ds(0, toks) if ref.shape[0] == toks else pl.ds(pl.multiple_of(side * toks, toks), toks)


def chunk_of(me, r):
    return me ^ (2 * STEPS[r % 4]) ^ (r // 4)


def inner_body(where, along, across, x, inner, t_l):
    me = where[0]
    toks = inner.shape[2]
    at = tokens_at(x, where[1], toks)
    masks = [jnp.concatenate([mask, mask], axis=1) for mask in unit_masks()]
    for r in range(CHUNKS):
        piece = (along, across)[r // 4]
        for gg in range(8):
            t_l[gg, rows(chunk_of(me, r)), :] = piece[r % 4, pl.ds(gg * 16, 16), :]

    def step(i, _):
        both = jnp.concatenate([t_l[i], t_l[4 + i]], axis=1)
        total = jnp.zeros((toks, 256), f32)
        for p in range(GROUP // 2):
            w = jnp.concatenate([both * masks[2 * p + h] for h in range(2)], axis=0)
            total += nn(x[at, lanes(i * GROUP // 2 + p, 256)], w)
        for gu in range(2):
            inner[gu, rows(i, 128), :] = rounded(total[:, gu * 128 : (gu + 1) * 128].T)
        return 0

    lax.fori_loop(0, 4, step, 0, unroll=4)


def by_parity(ref, m):
    return jnp.concatenate(
        [ref[pl.ds(m, 8, stride=2 * NB), :], ref[pl.ds(m + NB, 8, stride=2 * NB), :]], axis=0
    ).astype(bf16)


def middle_body(
    scale, where, order, own_a, own_b, oth_a, oth_b, inner_own, inner_oth, y, y_got, keep, send,
    inner, ret, t_r, n_ld, act_own, act_oth, slope_own, slope_oth,
    r_lo, r_hi, s_rd, n_r, n_rd, t_rd, t_ld, g_out, down, hid_s,
):
    me, side = where[0], where[1]
    toks = inner.shape[1]
    ats = [tokens_at(v, side, toks) for v in (y, y_got)]
    masks = unit_masks()
    s_r = (r_lo, r_hi)
    for gu in range(2):
        for b, part in enumerate([inner_own, inner_oth]):
            inner[rows(gu * 2 + (side ^ b), 512), :] = part[gu]

    for b, pieces in enumerate([(own_a, own_b), (oth_a, oth_b)]):
        blk = side ^ b
        for r in range(CHUNKS):
            d = chunk_of(me, r)
            ref, at = pieces[r // 4], r % 4
            for gu in range(2):
                for al in range(2):
                    row = pl.multiple_of((2 * d + al) * 128 + gu * NB + blk * HALF, HALF)
                    for half in range(2):
                        src = FIRST + half * 128 + gu * 64 + al * HALF
                        s_r[half][pl.ds(row, HALF), :] = ref[at, pl.ds(src, HALF), :].astype(f32)
            for al in range(2):
                row = pl.multiple_of((2 * d + al) * NB + blk * HALF, HALF)
                s_rd[pl.ds(row, HALF), :] = ref[at, pl.ds(FIRST + RD_AT + al * HALF, HALF), :].astype(f32)
            for g in range(4):
                t_ld[blk * 4 + g, rows(d, 32), :] = ref[at, pl.ds(FIRST + LD_AT + g * 32, 32), :]

    def stacked(ref, start, stride, g):
        return jnp.concatenate(
            [ref[pl.ds(start + g * GROUP + u, RANK, stride=stride), :] for u in range(GROUP)], axis=0
        )

    def turn(g, _):
        for gu in range(2):
            for h in range(2):
                flat = stacked(s_r[h], gu * NB, 128, g)
                n_r[gu, g, :, pl.ds(h * 128, 128)] = flat.astype(bf16)
                t_r[gu, g, pl.ds(h * 128, 128), :] = flat.astype(bf16).T
        for h in range(2):
            n_ld[g, :, pl.ds(h * 128, 128)] = t_ld[g, pl.ds(h * 128, 128), :].T
        flat = stacked(s_rd, 0, NB, g)
        n_rd[g] = flat.astype(bf16)
        t_rd[g] = flat.astype(bf16).T
        return 0

    lax.fori_loop(0, GROUPS, turn, 0)

    def blocks(g):
        return [(u, g * GROUP + u) for u in range(GROUP)]

    def second(i, _, b):
        g = (side ^ b) * 4 + i
        act_s, slope_s = ((act_own, slope_own), (act_oth, slope_oth))[b]
        turned = []
        for gu in range(2):
            mixed = [inner[pl.ds(gu * 1024 + order[k], RANK, stride=NB), :] for u, k in blocks(g)]
            turned.append(jnp.concatenate(mixed, axis=0).T.astype(bf16))
        span = pl.ds(pl.multiple_of(i * GROUP, GROUP), GROUP)
        act_s[span] = nn(spread(turned[0], masks), n_r[0, g]).reshape(GROUP, toks, WIDE)
        slope_s[span] = nn(spread(turned[1], masks), n_r[1, g]).reshape(GROUP, toks, WIDE)
        for u, k in blocks(g):
            local = i * GROUP + u
            gate, upper = act_s[local], slope_s[local]
            sig = 0.5 * jnp.tanh(0.5 * gate) + 0.5
            act = gate * sig
            act_s[local] = act
            slope_s[local] = upper * (sig + act * (1.0 - sig))
            hid_s[k] = (act * upper).astype(bf16)
        hidden = hid_s[pl.ds(pl.multiple_of(g * GROUP, GROUP), GROUP)].reshape(GROUP * toks, WIDE)
        total = chosen(nn(hidden, t_ld[g]), toks)
        down[rows(g, 128), :] = rounded(total.T)
        return 0

    for b in range(2):
        lax.fori_loop(0, 4, functools.partial(second, b=b), 0, unroll=4)

    def put(b, base, value):
        for al in range(2):
            g_out[b, pl.ds(base + al * HALF, 8, stride=DOWN), :] = value[al * 8 : (al + 1) * 8]

    for b in range(2):

        def third(i, _, b=b):
            g = (side ^ b) * 4 + i
            dms = [down[pl.ds(order[k], RANK, stride=NB), :] for u, k in blocks(g)]
            turned = jnp.concatenate(dms, axis=0).T.astype(bf16)
            student = nn(spread(turned, masks), n_rd[g])
            deltas = []
            for u, k in blocks(g):
                target = (y, y_got)[b][ats[b], lanes(i * GROUP + u)].astype(f32)
                part = student[u * toks : (u + 1) * toks]
                deltas.append(((part - target) * scale).astype(bf16))
            total = chosen(nn(jnp.concatenate(deltas, axis=0), t_rd[g]), toks)
            parity = [by_parity(down, order[k]) for u, k in blocks(g)]
            for q in range(2):
                d = deltas[4 * q : 4 * q + 4]
                m = parity[4 * q : 4 * q + 4]
                grads = nn(
                    crossed_pair(jnp.concatenate(m[:2], axis=0), jnp.concatenate(m[2:], axis=0)),
                    jnp.concatenate([jnp.concatenate(d[:2], axis=1), jnp.concatenate(d[2:], axis=1)], axis=0),
                )
                for e in range(4):
                    part = grads[e * RANK : (e + 1) * RANK, (e % 2) * 128 : (e % 2 + 1) * 128]
                    put(b, i * GROUP + 4 * q + e, part)
            total = rounded(total.T)
            for u, k in blocks(g):
                ret[pl.ds(order[k], RANK, stride=NB), :] = total[u * RANK : (u + 1) * RANK]
            return 0

        lax.fori_loop(0, 4, third, 0, unroll=4)

    def inward(i, _, b):
        g = (side ^ b) * 4 + i
        returned = ret[rows(g, 128), :].astype(bf16)
        grads = []
        for p in range(GROUP // 2):
            pair = [returned[u * RANK : (u + 1) * RANK] for u in (2 * p, 2 * p + 1)]
            both = hid_s[pl.ds(g * GROUP + 2 * p, 2)].reshape(2 * toks, WIDE)
            grads.append(nn(crossed_pair(*pair), both))
        grads = jnp.concatenate(grads, axis=0)
        for h in range(2):
            part = grads[:, h * 128 : (h + 1) * 128].T
            for q in range(4):
                at = (h * 4 + q) * DOWN + 64 + i * 32
                g_out[b, pl.ds(pl.multiple_of(at, 32), 32), :] = part[q * 32 : (q + 1) * 32]
        return 0

    for b in range(2):
        lax.fori_loop(0, 4, functools.partial(inward, b=b), 0, unroll=4)

    for b, out in enumerate([keep, send]):
        for r in range(CHUNKS):
            out[r] = g_out[b, rows(chunk_of(me, r), DOWN), :].astype(bf16)


def right_body(b, where, order, inner, ret, t_r, n_ld, act_s, slope_s, *refs):
    if b == 0:
        before, grads_out, back, g_out = refs
        back[...] = before[...]
    else:
        grads_out, back, g_out = refs
    me, side = where[0], where[1]
    toks = inner.shape[1]
    masks = unit_masks()

    def step(i, _):
        g = (side ^ b) * 4 + i
        blocks = [(u, g * GROUP + u) for u in range(GROUP)]
        turned = ret[rows(g, 128), :].T.astype(bf16)
        dhidden = nn(spread(turned, masks), n_ld[g])
        sent = ([], [])
        for u, j in blocks:
            local, part = i * GROUP + u, dhidden[u * toks : (u + 1) * toks]
            sent[0].append((part * slope_s[local]).astype(bf16))
            sent[1].append((part * act_s[local]).astype(bf16))
        for gu in range(2):
            total = rounded(chosen(nn(jnp.concatenate(sent[gu], axis=0), t_r[gu, g]), toks).T)
            for u, j in blocks:
                back[pl.ds(gu * 1024 + order[j], RANK, stride=NB), :] = total[u * RANK : (u + 1) * RANK]
        for u, j in blocks:
            mixed = [by_parity(inner, gu * 1024 + order[j]) for gu in range(2)]
            grad = nn(crossed_pair(*mixed), jnp.concatenate([sent[0][u], sent[1][u]], axis=0))
            for gu in range(2):
                for h in range(2):
                    base = h * 128 + gu * 64 + i * GROUP + u
                    for al in range(2):
                        g_out[pl.ds(base + al * HALF, 8, stride=RIGHT), :] = grad[
                            gu * RANK + al * 8 : gu * RANK + (al + 1) * 8, h * 128 : (h + 1) * 128
                        ]
        return 0

    lax.fori_loop(0, 4, step, 0, unroll=4)
    for r in range(CHUNKS):
        grads_out[r] = g_out[rows(chunk_of(me, r), RIGHT), :].astype(bf16)


def left_body(where, back, x, x_got, keep, send, turned):
    me, side = where[0], where[1]
    toks = back.shape[1]
    ats = [tokens_at(v, side, toks) for v in (x, x_got)]
    for b, (ref, out) in enumerate([(x, keep), (x_got, send)]):

        def step(i, _, b=b, ref=ref):
            parts = ([], [])
            for q in range(2):
                both = []
                for u in range(4 * q, 4 * q + 4):
                    j = ((side ^ b) * 4 + i) * GROUP + u
                    both += [back[rows(j), :], back[rows(j + NB), :]]
                both = jnp.concatenate(both, axis=0).astype(bf16)
                at = i * 4 + 2 * q
                x4 = jnp.concatenate([ref[ats[b], lanes(at, 256)], ref[ats[b], lanes(at + 1, 256)]], axis=0)
                grads = nn(crossed_pair(both[:64], both[64:]), x4)
                for e in range(4):
                    for gu in range(2):
                        top = (e * 2 + gu) * RANK
                        parts[gu].append(grads[top : top + RANK, (e % 2) * 128 : (e % 2 + 1) * 128])
            for gu in range(2):
                turned[rows(gu * 4 + i, 128), :] = jnp.concatenate(parts[gu], axis=0).T.astype(bf16)
            return 0

        lax.fori_loop(0, 4, step, 0, unroll=4)
        for r in range(CHUNKS):
            d = chunk_of(me, r)
            for gg in range(8):
                at = pl.multiple_of(gg * 128 + d * 16, 16)
                out[r, pl.ds(gg * 16, 16), :] = turned[pl.ds(at, 16), :]


VMEM = pl.BlockSpec(memory_space=pltpu.VMEM)
SMEM = pl.BlockSpec(memory_space=pltpu.SMEM)


ANY = pl.BlockSpec(memory_space=pl.ANY)
HBM = pl.BlockSpec(memory_space=pltpu.HBM)
VMEM_MIDDLE = 20 * 2**20
VMEM_RIGHT = 10 * 2**20


def prepare_call(factors):
    return pl.pallas_call(
        prepare_body,
        out_shape=jax.ShapeDtypeStruct((FIRST + REST, 128), bf16),
        in_specs=[HBM] * 6,
        out_specs=VMEM,
        scratch_shapes=[pltpu.VMEM(v.shape, bf16) for v in factors] + [pltpu.SemaphoreType.DMA((6,))],
        compiler_params=pltpu.CompilerParams(vmem_limit_bytes=60 * 2**20),
    )(*factors)


def finish_call(first, rights, downs):
    cut, count = len(first), len(first) + len(rights) + len(downs)
    turn = cut + len(rights)
    shapes = [256, 448, 256, 448, 448, 256]
    return pl.pallas_call(
        lambda *refs: finish_body(refs[:cut], refs[cut:turn], refs[turn:count], *refs[count:]),
        out_shape=tuple(jax.ShapeDtypeStruct((HALF, c), f32) for c in shapes),
        in_specs=[VMEM] * count,
        out_specs=(VMEM,) * 6,
        compiler_params=pltpu.CompilerParams(vmem_limit_bytes=16 * 2**20),
    )(*first, *rights, *downs)


def inner_call(where, along, across, x, toks):
    front = pl.BlockSpec((4, FIRST, 128), lambda i: (0, 0, 0))
    return pl.pallas_call(
        inner_body,
        grid=(1,),
        out_shape=jax.ShapeDtypeStruct((2, NB * RANK // 2, toks), f32),
        in_specs=[SMEM, front, front, VMEM],
        out_specs=VMEM,
        scratch_shapes=[pltpu.VMEM((8, BIN, 128), bf16)],
        compiler_params=pltpu.CompilerParams(vmem_limit_bytes=10 * 2**20),
        cost_estimate=pl.CostEstimate(flops=10**9, bytes_accessed=10**7, transcendentals=0),
    )(where, along, across, x)


def middle_call(scale, where, order, pieces, inner, y, y_got):
    toks = y_got.shape[0] // 2
    down = jax.ShapeDtypeStruct((CHUNKS, DOWN, 128), bf16)
    kept = jax.ShapeDtypeStruct((HALF, toks, WIDE), f32)
    return pl.pallas_call(
        functools.partial(middle_body, scale),
        out_shape=(
            down,
            down,
            jax.ShapeDtypeStruct((2 * NB * RANK, toks), f32),
            jax.ShapeDtypeStruct((NB * RANK, toks), f32),
            jax.ShapeDtypeStruct((2, GROUPS, WIDE, 128), bf16),
            jax.ShapeDtypeStruct((GROUPS, 128, WIDE), bf16),
            kept,
            kept,
            kept,
            kept,
        ),
        in_specs=[SMEM, SMEM] + [VMEM] * 8,
        out_specs=(VMEM,) * 10,
        scratch_shapes=[
            pltpu.VMEM((RANK * 128, 128), f32),
            pltpu.VMEM((RANK * 128, 128), f32),
            pltpu.VMEM((RANK * NB, 128), f32),
            pltpu.VMEM((2, GROUPS, 128, WIDE), bf16),
            pltpu.VMEM((GROUPS, 128, BIN), bf16),
            pltpu.VMEM((GROUPS, BIN, 128), bf16),
            pltpu.VMEM((GROUPS, WIDE, 128), bf16),
            pltpu.VMEM((2, CHUNKS * DOWN, 128), f32),
            pltpu.VMEM((NB * RANK, toks), f32),
            pltpu.VMEM((NB, toks, WIDE), bf16),
        ],
        compiler_params=pltpu.CompilerParams(vmem_limit_bytes=VMEM_MIDDLE),
        cost_estimate=pl.CostEstimate(flops=5 * 10**9, bytes_accessed=4 * 10**7, transcendentals=0),
    )(where, order, *pieces, *inner, y, y_got)


def right_call(b, where, order, *arrays):
    toks = arrays[0].shape[1]
    return pl.pallas_call(
        functools.partial(right_body, b),
        out_shape=(
            jax.ShapeDtypeStruct((CHUNKS, RIGHT, 128), bf16),
            jax.ShapeDtypeStruct((2 * NB * RANK, toks), f32),
        ),
        in_specs=[SMEM, SMEM] + [VMEM] * len(arrays),
        out_specs=(VMEM, VMEM),
        scratch_shapes=[pltpu.VMEM((CHUNKS * RIGHT, 128), f32)],
        compiler_params=pltpu.CompilerParams(vmem_limit_bytes=VMEM_RIGHT),
        cost_estimate=pl.CostEstimate(flops=5 * 10**9, bytes_accessed=2 * 10**7, transcendentals=0),
    )(where, order, *arrays)


def left_call(where, back, x, x_got):
    grads = jax.ShapeDtypeStruct((CHUNKS, FIRST, 128), bf16)
    return pl.pallas_call(
        left_body,
        out_shape=(grads, grads),
        in_specs=[SMEM] + [VMEM] * 3,
        out_specs=(VMEM, VMEM),
        scratch_shapes=[
            pltpu.VMEM((8 * 128, 128), bf16),
        ],
        compiler_params=pltpu.CompilerParams(vmem_limit_bytes=16 * 2**20),
        cost_estimate=pl.CostEstimate(flops=10**9, bytes_accessed=10**7, transcendentals=0),
    )(where, back, x, x_got)


def swap(v, axis, bit, size):
    return lax.ppermute(v, axis, [(i, i ^ bit) for i in range(size)])


def sibling(v):
    return swap(v, "blk", 1, 2)


def gathered(mine, n):
    z1, z2, z3 = [swap(mine, "dp", 2 * s, n) for s in range(1, 4)]
    x0, x1, x2, x3 = [swap(v, "dp", 1, n) for v in (mine, z1, z2, z3)]
    pair = (x0, x1)
    along = jnp.stack([mine, z2, z1, z3])
    across = jnp.stack([pair[0], x2, pair[1], x3])
    return along, across, sibling(along), sibling(across)


def add(a, b):
    return (a.astype(f32) + b.astype(f32)).astype(bf16)


def tie(value, *others):
    return lax.optimization_barrier((value,) + others)[0]


def over_x(keep, got, n):
    away = add(keep[4:], got[4:])
    return away, swap(away, "dp", 1, n)


def line_of(keep, got, crossed):
    return (keep[:4].astype(f32) + got[:4].astype(f32) + crossed.astype(f32)).astype(bf16)


def over_z(line, n):
    return add(line[:2], swap(line[2:], "dp", 2, n))


def on_device(activations, teacher_out, block_order, *factors):
    n = lax.axis_size("dp")
    me = lax.axis_index("dp")
    side = lax.axis_index("blk")
    toks = activations.shape[0] // 2
    scale = float(activations.shape[0] * n) ** (-0.5)
    direct = n == CHUNKS
    if direct:
        where = jnp.stack([me, side]).astype(jnp.int32)
        pieces = gathered(prepare_call(factors), n)
    else:
        where = jnp.stack([jnp.zeros_like(side), side]).astype(jnp.int32)
        whole = [lax.all_gather(v, "dp", axis=1, tiled=True) for v in factors]
        cut = [jnp.moveaxis(v.reshape(HALF, CHUNKS, -1), 1, 0) for v in whole]
        packed = jnp.concatenate(jax.vmap(pack)(*cut), axis=1)
        packed = packed.reshape((4, 2) + packed.shape[1:])[jnp.array(STEPS)]
        pieces = (packed[:, 0], packed[:, 1], sibling(packed[:, 0]), sibling(packed[:, 1]))
    x, y = [lax.dynamic_slice_in_dim(v, side * toks, toks, 0) for v in (activations, teacher_out)]
    x_got, y_got = sibling(activations), sibling(teacher_out)
    inner = (
        inner_call(where, pieces[0], pieces[1], x, toks),
        inner_call(where, pieces[2], pieces[3], x_got, toks),
    )
    keep, send, *state = middle_call(scale, where, block_order, pieces, inner, y, y_got)
    shared, (act_own, act_oth, slope_own, slope_oth) = state[:4], state[4:]
    got = sibling(send)
    right_send, back = right_call(1, where, block_order, *shared, act_oth, slope_oth)
    right_got = sibling(right_send)
    if direct:
        away, crossed = over_x(keep, tie(got, back), n)
        back = tie(back, away)
    right_keep, back = right_call(0, where, block_order, *shared, act_own, slope_own, back)
    if direct:
        right_away, right_crossed = over_x(right_keep, right_got, n)
        back = tie(back, right_away)
    left_keep, left_send = left_call(where, back, x, x_got)
    left_got = sibling(left_send)
    if direct:
        half = over_z(line_of(keep, got, crossed), n)
        left_away = add(left_keep[4:], left_got[4:])
        left_crossed = swap(left_away, "dp", 1, n)
        right_half = over_z(tie(line_of(right_keep, right_got, right_crossed), left_away), n)
        down = [half[0], swap(half[1], "dp", 4, n)]
        left_half = over_z(line_of(left_keep, left_got, left_crossed), n)
        right = [right_half[0], swap(tie(right_half[1], half), "dp", 4, n)]
        left = [left_half[0], swap(tie(left_half[1], right_half), "dp", 4, n)]
        return finish_call(left, right, down)
    rest = (jnp.concatenate([right_keep, keep], axis=1), jnp.concatenate([right_got, got], axis=1))
    sums = []
    rest = [jnp.concatenate(v, axis=1) for v in ((right_keep, keep), (right_send, send))]
    for own, away in ((left_keep, left_got), rest):
        total = own.astype(f32) + away.astype(f32)
        ranks = jnp.array(STEPS)
        sums.append(jnp.stack([total[:4][ranks], total[4:][ranks]], axis=1).reshape(total.shape))
    parts = jax.vmap(unpack)(*sums)
    parts = [jnp.moveaxis(v, 0, 1).reshape(HALF, -1) for v in parts]
    return tuple(lax.psum_scatter(v, "dp", scatter_dimension=1, tiled=True) for v in parts)


def solution(mesh):
    tokens = P(("group", "dp"), "blk")
    factor = P("blk", "dp")
    grad = P(("group", "blk"), "dp")
    return jax.shard_map(
        on_device,
        mesh=mesh,
        in_specs=(tokens, tokens, P()) + (factor,) * 6,
        out_specs=(grad,) * 6,
        check_vma=False,
    )
```
